512 devices in a mesh: term: 16 (over z, core), block: 32 (over y, x).
Axes of the slice: x: 4, y: 8, z: 8, core: 2. Of those that a mesh axis runs over, the one named last changes fastest.
Arguments:
- start: float32 [32, 256, 256], P('block'), may hold values from -6 to 6
- diagonal: float32 [32, 256, 256], P('block'), may hold values from -0.5 to 5
- left_ops: float32 [64, 32, 256, 256], P('term', 'block'), as said below
- right_ops: float32 [64, 32, 256, 256], P('term', 'block')
- offsets: int32 [64, 32], P('term', 'block'), may hold values from -1 to 1, as said below
- sizes: int32 [32], P('block'), may hold values from 128 to 256, as said below
Outputs:
- wave: float32 [32, 256, 256], P('block')
- image: float32 [32, 256, 256], P('block')
- energies: float32 [3], replicated
The draws below stay inside these ranges and needn't reach their ends.
Inputs may be any that keep to these rules, and one draw needn't show every extreme that they name: `sizes`: each entry is 128 or 256; both occur in every draw. `offsets`: each term has one offset for all blocks; term 0 has offset 1 and term 1 offset 0; term t + 32 has the opposite offset of term t. For t < 32 with offset o, left_ops[t + 32, c] is the transpose of left_ops[t, c + o] wherever c + o is a block; likewise right_ops, so that H is symmetric.
All inputs are finite; a program needn't handle non-finite values.
Results may differ from the reference program's by a relative error of at most 0.0003.
Values sent between devices are 32-bit elements; how exact they have to be, the bound alone decides.
No kernel may reach another device: no remote copies, remote signals or barrier semaphores. Data moves between devices by JAX's collectives and lax.ppermute only.
A program may use at most 64 MiB of HBM per device.

```python
import math
import jax
import jax.numpy as jnp
from jax import lax

M = 256
ITERS = 3
TERMS = 64
BLOCKS = 32


def half_offsets(key):
    first = jax.random.randint(jax.random.fold_in(key, 101), (TERMS // 2,), -1, 2)
    return first.at[0].set(1).at[1].set(0).astype(jnp.int32)


def profiles(key):
    low = math.log(0.35)
    high = math.log(1.5)
    row_part = jnp.exp(jax.random.uniform(jax.random.fold_in(key, 202), (BLOCKS, M), jnp.float32, low, high))
    col_part = jnp.exp(jax.random.uniform(jax.random.fold_in(key, 203), (BLOCKS, M), jnp.float32, low, high))
    return (row_part, col_part)


def draw_offsets(key, part):
    first = half_offsets(key)
    whole = jnp.concatenate([first, -first], axis=0)
    return jnp.broadcast_to(whole[:, None], (TERMS, BLOCKS)).astype(jnp.int32)


def draw_diagonal(key, part):
    row_part, col_part = profiles(key)
    key = jax.random.fold_in(key, 44)
    noise = jax.random.uniform(key, (BLOCKS, M, M), jnp.float32, -0.25, 0.25)
    return 2.0 * row_part[:, :, None] * col_part[:, None, :] + noise


def draw_left_ops(key, part):
    row_part, col_part = profiles(key)
    inner = jax.random.fold_in(key, 21)
    inner = jax.random.fold_in(inner, 0)
    return paired_ops_keyed(key, inner, (M * TERMS) ** (-0.5), row_part)


def draw_right_ops(key, part):
    row_part, col_part = profiles(key)
    inner = jax.random.fold_in(key, 33)
    return paired_ops_keyed(key, inner, M ** (-0.5), col_part)


def paired_ops_keyed(base_key, value_key, spread, profile):
    first = half_offsets(base_key)
    base = jax.random.normal(value_key, (TERMS // 2, BLOCKS, M, M), jnp.float32)
    identity = jnp.eye(M, dtype=jnp.float32)
    steady = base[1] * (0.5 * M ** (-0.5)) + profile[:, :, None] * identity[None, :, :]
    base = (base * spread).at[1].set(steady)
    index = jnp.clip(jnp.arange(BLOCKS, dtype=jnp.int32)[None, :] + first[:, None], 0, BLOCKS - 1)
    moved = jax.vmap(lambda table, rows: table[rows])(base, index)
    mirror = jnp.swapaxes(moved, 2, 3)
    return jnp.concatenate([base, mirror], axis=0)


def draw_sizes(key, part):
    key = jax.random.fold_in(key, 11)
    unit_count = jax.random.randint(key, (BLOCKS,), 1, 3)
    unit_count = unit_count.at[0].set(2).at[1].set(1)
    return (unit_count * (M // 2)).astype(jnp.int32)


def block_scale(key, extent, pieces, least, high):
    loudness, own = 1.0, jax.random.fold_in(key, 6)
    for dim, parts in pieces:
        draws = jnp.exp(jax.random.uniform(jax.random.fold_in(own, dim), (parts,), jnp.float32, least / len(pieces), high / len(pieces)))
        loudness = loudness * jnp.repeat(draws, extent[dim] // parts).reshape([-1 if axis == dim else 1 for axis in range(len(extent))])
    return loudness


def gaussian(key, extent, scale, limit, shards=(), kind=jnp.bfloat16):
    loudness = block_scale(key, extent, shards, -0.22, 0.18) if shards else 1.0
    array = jax.random.normal(key, extent, jnp.float32) * scale * loudness
    return jnp.minimum(jnp.maximum(array, -limit), limit).astype(kind)


def setup_inputs(seed: int = 0) -> dict:
    arg_keys = jax.random.split(jax.random.key(seed), 7)
    return {
        "start": gaussian(arg_keys[0], (BLOCKS, M, M), 1.0, 6.0, ((0, 32),), jnp.float32),
        "diagonal": draw_diagonal(jax.random.fold_in(arg_keys[6], 71), 0),
        "left_ops": draw_left_ops(jax.random.fold_in(arg_keys[6], 71), 0),
        "right_ops": draw_right_ops(jax.random.fold_in(arg_keys[6], 71), 0),
        "offsets": draw_offsets(jax.random.fold_in(arg_keys[6], 71), 0),
        "sizes": draw_sizes(jax.random.fold_in(arg_keys[6], 71), 0),
    }


def hamiltonian(vector, left_ops, right_ops, offsets, live_mask):
    padded = jnp.pad(vector, ((1, 1), (0, 0), (0, 0)))
    blocks = jnp.arange(vector.shape[0], dtype=jnp.int32)

    def one_term(running, inputs):
        left_op, right_op, offset_row = inputs
        source = padded[(blocks + 1 - offset_row).astype(jnp.int32)]
        left_half = jnp.einsum('bij,bjk->bik', left_op, source, precision=lax.Precision.HIGHEST)
        return (running + jnp.einsum('bik,bkl->bil', left_half, right_op, precision=lax.Precision.HIGHEST), None)
    running, unused = lax.scan(one_term, jnp.zeros(vector.shape, jnp.float32), (left_ops, right_ops, offsets))
    return running * live_mask

def reference(start, diagonal, left_ops, right_ops, offsets, sizes):
    tile_rows = start.shape[1]
    live_rows = (jnp.arange(tile_rows, dtype=jnp.int32)[None, :] < sizes[:, None]).astype(jnp.float32)
    live_mask = live_rows[:, :, None] * live_rows[:, None, :]
    initial = start * live_mask
    vector = initial / jnp.sqrt(jnp.sum(initial * initial) + 1e-12)
    image_vec = hamiltonian(vector, left_ops, right_ops, offsets, live_mask)
    energies = []
    for iteration in range(ITERS):
        rayleigh = jnp.sum(vector * image_vec)
        residual = image_vec - rayleigh * vector
        trial_vec = residual / jnp.maximum(jnp.abs(diagonal - rayleigh), 1.0)
        projection = jnp.sum(vector * trial_vec)
        orthogonal = trial_vec - projection * vector
        unit_vec = orthogonal / jnp.sqrt(jnp.sum(orthogonal * orthogonal) + 1e-12)
        image_unit = hamiltonian(unit_vec, left_ops, right_ops, offsets, live_mask)
        coupling = jnp.sum(unit_vec * image_vec)
        curvature = jnp.sum(unit_vec * image_unit)
        lowest = 0.5 * (rayleigh + curvature) - jnp.sqrt((0.5 * (rayleigh - curvature)) ** 2 + coupling * coupling)
        gap_value = curvature - lowest
        length = jnp.sqrt(gap_value * gap_value + coupling * coupling)
        vector = (gap_value * vector - coupling * unit_vec) / length
        image_vec = (gap_value * image_vec - coupling * image_unit) / length
        energies.append(lowest)
    factor = jnp.sqrt(jnp.float32(BLOCKS * M * M))
    return (vector * factor, image_vec * factor, jnp.stack(energies))
```

```python
import math

import jax
import jax.numpy as jnp
import numpy as np
from jax import lax
from jax.experimental import pallas as pl
from jax.experimental.pallas import tpu as pltpu
from jax.sharding import Mesh, PartitionSpec as P

ITERS = 3
ZS, CORES, BLOCKS = 8, 2, 32
GROUP = ZS * CORES
M = 256
PIECE = M // ZS
HALF = PIECE // CORES
SCAL = 8
TERM = ("z", "core")
ALL = ("z", "core", "block")
VMEM = pl.BlockSpec(memory_space=pltpu.VMEM)
SMEM = pl.BlockSpec(memory_space=pltpu.SMEM)
BF16, F32 = jnp.bfloat16, jnp.float32


def split(x):
    high = x.astype(BF16)
    return high, (x - high.astype(F32)).astype(BF16)


def dot3(a, b):
    def mm(x, y):
        return lax.dot_general(x, y, (((1,), (0,)), ((), ())), preferred_element_type=F32)

    return mm(a[0], b[0]) + (mm(a[0], b[1]) + mm(a[1], b[0]))


def column_sum(x):
    return jnp.sum(x, axis=0, keepdims=True)


def apply_terms(info, left, right, t_high, t_low, t_own, v_own, r_own, part):
    total = jnp.zeros((M, M), F32)
    for term in range(left.shape[0]):
        sel = 1 - info[2 + term]
        half = dot3(split(left[term]), (t_high[sel], t_low[sel]))
        total = total + dot3(split(half), split(right[term]))
    size = info[1]
    live = (lax.broadcasted_iota(jnp.int32, (M, M), 0) < size) & (
        lax.broadcasted_iota(jnp.int32, (M, M), 1) < size
    )
    total = jnp.where(live, total, 0.0)
    share = 1.0 / GROUP
    rows = [
        column_sum(t_own * t_own) * share,
        column_sum(t_own * total),
    ]
    if v_own is not None:
        rows += [
            column_sum(v_own * t_own) * share,
            column_sum(t_own * r_own) * share,
            column_sum(v_own * total),
        ]
    rows.append(jnp.zeros((SCAL - len(rows), M), F32))
    scal = jnp.concatenate(rows, axis=0)
    for z in range(ZS):
        part[z, :PIECE] = total[z * PIECE : (z + 1) * PIECE]
        part[z, PIECE:] = scal


def first_kernel(info, left, right, x3, part, t_high, t_low):
    for i in range(3):
        t_high[i], t_low[i] = split(x3[i])
    apply_terms(info, left, right, t_high, t_low, x3[1], None, None, part)


def global_sums(info, gathered, row):
    shift = lax.shift_right_logical(info[0], 1)
    total = None
    for m in range(GROUP):
        piece = gathered[lax.rem(m + GROUP - shift, GROUP), row : row + SCAL]
        total = piece if total is None else total + piece
    return jnp.sum(total, axis=1, keepdims=True)


def scalars(first, sums, state):
    tt, th = sums[0:1], sums[1:2]
    if first:
        scale = tt + 1e-12
        return None, jnp.sqrt(scale), None, None, None, th / scale, tt / scale, None
    p, tr, vh = sums[2:3], sums[3:4], sums[4:5]
    rho, vv = state[0:1, 0:1], state[1:2, 0:1]
    norm_sq = jnp.maximum(tt - 2.0 * p * p + p * p * vv, 0.0)
    n_sq = norm_sq + 1e-12
    n = jnp.sqrt(n_sq)
    tw = tr + rho * p
    coupling = tr / n
    curvature = (th - p * tw - p * vh + p * p * rho) / n_sq
    lowest = 0.5 * (rho + curvature) - jnp.sqrt((0.5 * (rho - curvature)) ** 2 + coupling * coupling)
    gap = curvature - lowest
    len_sq = gap * gap + coupling * coupling
    length = jnp.sqrt(len_sq)
    v_image = (vh - p * rho) / n
    v_unit = (p - p * vv) / n
    unit_sq = norm_sq / n_sq
    next_rho = (gap * gap * rho - gap * coupling * (v_image + coupling) + coupling * coupling * curvature) / len_sq
    next_vv = (gap * gap * vv - 2.0 * gap * coupling * v_unit + coupling * coupling * unit_sq) / len_sq
    return p, n, gap, coupling, length, next_rho, next_vv, lowest


def combine(first, scal, v, w, t, y):
    p, n, gap, coupling, length = scal[:5]
    if first:
        return t / n, y / n
    by_unit = coupling / (n * length)
    by_old = gap / length + p * by_unit
    return by_old * v - by_unit * t, by_old * w - by_unit * y


def state_rows(first, scal, state, iteration):
    rows = [scal[5], scal[6]]
    for i in range(ITERS):
        if i < iteration - 1:
            rows.append(state[2 + i : 3 + i, 0:1])
        elif i == iteration - 1 and not first:
            rows.append(scal[7])
        else:
            rows.append(jnp.zeros((1, 1), F32))
    rows.append(jnp.zeros((SCAL - len(rows), 1), F32))
    return jnp.broadcast_to(jnp.concatenate(rows, axis=0), (SCAL, 128))


def step_kernel(iteration, *refs):
    first = iteration == 0
    if first:
        info, left, right, diag3, gathered, t3, state_out, v_out, w_out, t_out, part, t_high, t_low = refs
        v3 = w3 = state = None
    else:
        (info, left, right, diag3, gathered, v3, w3, t3, state, state_out, v_out, w_out, t_out, part,
         t_high, t_low) = refs
    scal = scalars(first, global_sums(info, gathered, PIECE + HALF), None if first else state)
    rho = scal[5]
    state_out[...] = state_rows(first, scal, state, iteration)

    def update(block, rows, y):
        old = (None, None) if first else (v3[block, rows], w3[block, rows])
        v, w = combine(first, scal, *old, t3[block, rows], y)
        r = w - rho * v
        t = r / jnp.maximum(jnp.abs(diag3[block, rows] - rho), 1.0)
        v_out[block, rows] = v
        w_out[block, rows] = w
        t_out[block, rows] = t
        t_high[block, rows], t_low[block, rows] = split(t)

    for z in range(ZS):
        rows = pl.ds(z * PIECE, PIECE)
        update(0, rows, gathered[2 * z, :PIECE])
        update(2, rows, gathered[2 * z + 1, :PIECE])
        update(1, rows, jnp.concatenate(
            [gathered[2 * z, PIECE : PIECE + HALF], gathered[2 * z + 1, PIECE : PIECE + HALF]], axis=0))
    v_own = v_out[1]
    apply_terms(info, left, right, t_high, t_low, t_out[1], v_own, w_out[1] - rho * v_own, part)


def last_kernel(factor, info, gathered, v3, w3, t3, state, wave, image, state_out):
    scal = scalars(False, global_sums(info, gathered, HALF), state)
    state_out[...] = state_rows(False, scal, state, ITERS)
    for j in range(GROUP):
        rows = pl.ds(j * HALF, HALF)
        v, w = combine(False, scal, v3[0, rows], w3[0, rows], t3[0, rows], gathered[j, :HALF])
        wave[0, rows] = v * factor
        image[0, rows] = w * factor


def shape(*dims):
    return jax.ShapeDtypeStruct(dims, F32)


PARAMS = pltpu.CompilerParams(vmem_limit_bytes=24 * 1024 * 1024)
SPLITS = [pltpu.VMEM((3, M, M), BF16), pltpu.VMEM((3, M, M), BF16)]
PART = shape(ZS, PIECE + SCAL, M)


def run_first(info, left, right, x3):
    return pl.pallas_call(
        first_kernel,
        out_shape=PART,
        in_specs=[SMEM] + [VMEM] * 3,
        out_specs=VMEM,
        scratch_shapes=SPLITS,
        compiler_params=PARAMS,
        name="first",
    )(info, left, right, x3)


def run_step(iteration, info, *arrays):
    def body(*refs):
        step_kernel(iteration, *refs)

    return pl.pallas_call(
        body,
        out_shape=(shape(SCAL, 128), shape(3, M, M), shape(3, M, M), shape(3, M, M), PART),
        in_specs=[SMEM] + [VMEM] * len(arrays),
        out_specs=(VMEM,) * 5,
        scratch_shapes=SPLITS,
        compiler_params=PARAMS,
        name="step",
    )(info, *arrays)


def run_last(info, gathered, v3, w3, t3, state):
    factor = math.sqrt(BLOCKS * M * M)

    def body(*refs):
        last_kernel(factor, *refs)

    own = pl.BlockSpec((1, M, M), lambda i: (1, 0, 0))

    def whole(x):
        return pl.BlockSpec(x.shape, lambda i: (0,) * x.ndim)

    out = pl.BlockSpec((1, M, M), lambda i: (0, 0, 0))
    return pl.pallas_call(
        body,
        grid=(1,),
        out_shape=(shape(1, M, M), shape(1, M, M), shape(SCAL, 128)),
        in_specs=[SMEM, whole(gathered), own, own, own, whole(state)],
        out_specs=(out, out, whole(state)),
        compiler_params=PARAMS,
        name="last",
    )(info, gathered, v3, w3, t3, state)


def halo_pairs():
    pairs = []
    for z in range(ZS):
        for core in range(CORES):
            for b in range(BLOCKS):
                source = b - 1 if core == 0 else b + 1
                if 0 <= source < BLOCKS:
                    base = (z * CORES + core) * BLOCKS
                    pairs.append((base + source, base + b))
    return pairs


def spread_pairs(flip):
    return [
        (j * BLOCKS + ((b ^ flip) + 2 * j) % BLOCKS, j * BLOCKS + b)
        for j in range(GROUP)
        for b in range(BLOCKS)
    ]


def halo_whole(block):
    got = lax.ppermute(block, ALL, halo_pairs())
    both = lax.all_gather(got, "core", axis=0)
    return jnp.stack([both[0], block, both[1]])


def exchange(part, with_halo):
    pair = lax.all_gather(part, "core", axis=0)
    summed = pair[0] + pair[1]
    pieces = lax.all_to_all(summed, "z", 0, 0, tiled=True)
    mine = jnp.sum(pieces, axis=0)
    rows, scal = mine[:PIECE], mine[PIECE:]
    parts = []
    if with_halo:
        parts.append(lax.ppermute(rows, ALL, halo_pairs()))
    spread = lax.ppermute(scal, ALL, spread_pairs(0)) + lax.ppermute(scal, ALL, spread_pairs(1))
    parts.append(lax.dynamic_slice_in_dim(rows, lax.axis_index("core") * HALF, HALF, 0))
    parts.append(spread)
    return lax.all_gather(jnp.concatenate(parts, axis=0), TERM, axis=0)


def per_device(start, diagonal, left_ops, right_ops, offsets, sizes):
    left, right = left_ops[:, 0], right_ops[:, 0]
    info = jnp.concatenate([lax.axis_index("block")[None].astype(jnp.int32), sizes, offsets[:, 0]])
    live = jnp.arange(M, dtype=jnp.int32) < sizes[0]
    masked = jnp.where(live[:, None] & live[None, :], start[0], 0.0)
    x3 = halo_whole(masked)
    part = run_first(info, left, right, x3)
    diag3 = halo_whole(diagonal[0])
    gathered = exchange(part, True)
    state, v3, w3, t3, part = run_step(0, info, left, right, diag3, gathered, x3)
    for iteration in range(1, ITERS):
        gathered = exchange(part, True)
        state, v3, w3, t3, part = run_step(
            iteration, info, left, right, diag3, gathered, v3, w3, t3, state)
    gathered = exchange(part, False)
    wave, image, state = run_last(info, gathered, v3, w3, t3, state)
    return wave, image, state[2 : 2 + ITERS, 0]


def solution(mesh):
    grid = Mesh(np.asarray(mesh.devices).reshape(ZS, CORES, BLOCKS), ALL)
    return jax.shard_map(
        per_device,
        mesh=grid,
        in_specs=(
            P("block", None, None),
            P("block", None, None),
            P(TERM, "block", None, None),
            P(TERM, "block", None, None),
            P(TERM, "block"),
            P("block"),
        ),
        out_specs=(P("block", None, None), P("block", None, None), P()),
        check_vma=False,
    )
```

```python
import math

import jax
import jax.numpy as jnp
import numpy as np
from jax import lax
from jax.experimental import pallas as pl
from jax.experimental.pallas import tpu as pltpu
from jax.sharding import Mesh, PartitionSpec as P

ITERS = 3
ZS, CORES, BLOCKS = 8, 2, 32
GROUP = ZS * CORES
M = 256
PIECE = M // ZS
LANES = M // CORES
ROWS = PIECE * CORES
SCAL = 8
XS = 4
YS = BLOCKS // XS
TERM = ("z", "core")
ALL = ("z", "core", "block")
VMEM = pl.BlockSpec(memory_space=pltpu.VMEM)
SMEM = pl.BlockSpec(memory_space=pltpu.SMEM)
HBM = pl.BlockSpec(memory_space=pltpu.HBM)
BF16, F32 = jnp.bfloat16, jnp.float32


def split(x):
    high = x.astype(BF16)
    return high, (x - high.astype(F32)).astype(BF16)


def dot3(a, b):
    def mm(x, y):
        return lax.dot_general(x, y, (((1,), (0,)), ((), ())), preferred_element_type=F32)

    return mm(a[0], b[0]) + (mm(a[0], b[1]) + mm(a[1], b[0]))


def column_sum(x):
    folded = x[:, :LANES] + x[:, LANES:]
    return jnp.sum(folded, axis=0, keepdims=True)


def apply_terms(info, left, right, t_high, t_low, t_own, v_own, r_own, part):
    total = jnp.zeros((M, M), F32)
    for term in range(left.shape[0]):
        sel = 1 - info[2 + term]
        half = dot3(split(left[term]), (t_high[sel], t_low[sel]))
        total = total + dot3(split(half), split(right[term]))
    size = info[1]
    live = (lax.broadcasted_iota(jnp.int32, (M, M), 0) < size) & (
        lax.broadcasted_iota(jnp.int32, (M, M), 1) < size
    )
    total = jnp.where(live, total, 0.0)
    share = 1.0 / GROUP
    rows = [
        column_sum(t_own * t_own) * share,
        column_sum(t_own * total),
    ]
    if v_own is not None:
        rows += [
            column_sum(v_own * t_own) * share,
            column_sum(t_own * r_own) * share,
            column_sum(v_own * total),
        ]
    rows.append(jnp.zeros((SCAL - len(rows), LANES), F32))
    scal = jnp.concatenate(rows, axis=0)
    for z in range(ZS):
        for core in range(CORES):
            part[z, core * PIECE : (core + 1) * PIECE] = total[
                z * PIECE : (z + 1) * PIECE, core * LANES : (core + 1) * LANES]
        part[z, ROWS:] = scal


def first_kernel(info, left, right, x_own, x_side, part, t_high, t_low):
    t_high[0], t_low[0] = split(x_side[0])
    t_high[1], t_low[1] = split(x_own[...])
    t_high[2], t_low[2] = split(x_side[1])
    apply_terms(info, left, right, t_high, t_low, x_own[...], None, None, part)


def global_sums(info, gathered, row):
    y, x = lax.shift_right_logical(info[0], 2), info[0] & (XS - 1)
    total = None
    for block in range(BLOCKS):
        far = (block % XS - x) & (XS - 1)
        slot = lax.shift_right_logical(far, 1)
        z = (block // XS - y - slot * (YS // 2)) & (YS - 1)
        at = pl.ds(pl.multiple_of(row + SCAL * slot, SCAL), SCAL)
        piece = gathered[CORES * z + (far & 1), at]
        total = piece if total is None else total + piece
    return jnp.sum(total, axis=1, keepdims=True)


def scalars(first, sums, state):
    tt, th = sums[0:1], sums[1:2]
    if first:
        scale = tt + 1e-12
        return None, jnp.sqrt(scale), None, None, None, th / scale, tt / scale, None
    p, tr, vh = sums[2:3], sums[3:4], sums[4:5]
    rho, vv = state[0:1, 0:1], state[1:2, 0:1]
    norm_sq = jnp.maximum(tt - 2.0 * p * p + p * p * vv, 0.0)
    n_sq = norm_sq + 1e-12
    n = jnp.sqrt(n_sq)
    tw = tr + rho * p
    coupling = tr / n
    curvature = (th - p * tw - p * vh + p * p * rho) / n_sq
    lowest = 0.5 * (rho + curvature) - jnp.sqrt((0.5 * (rho - curvature)) ** 2 + coupling * coupling)
    gap = curvature - lowest
    len_sq = gap * gap + coupling * coupling
    length = jnp.sqrt(len_sq)
    v_image = (vh - p * rho) / n
    v_unit = (p - p * vv) / n
    unit_sq = norm_sq / n_sq
    next_rho = (gap * gap * rho - gap * coupling * (v_image + coupling) + coupling * coupling * curvature) / len_sq
    next_vv = (gap * gap * vv - 2.0 * gap * coupling * v_unit + coupling * coupling * unit_sq) / len_sq
    return p, n, gap, coupling, length, next_rho, next_vv, lowest


def combine(first, scal, v, w, t, y):
    p, n, gap, coupling, length = scal[:5]
    if first:
        return t / n, y / n
    by_unit = coupling / (n * length)
    by_old = gap / length + p * by_unit
    return by_old * v - by_unit * t, by_old * w - by_unit * y


def state_rows(first, scal, state, iteration):
    rows = [scal[5], scal[6]]
    for i in range(ITERS):
        if i < iteration - 1:
            rows.append(state[2 + i : 3 + i, 0:1])
        elif i == iteration - 1 and not first:
            rows.append(scal[7])
        else:
            rows.append(jnp.zeros((1, 1), F32))
    rows.append(jnp.zeros((SCAL - len(rows), 1), F32))
    return jnp.broadcast_to(jnp.concatenate(rows, axis=0), (SCAL, 128))


def trial(v, w, diag, rho):
    r = w - rho * v
    return r, r / jnp.maximum(jnp.abs(diag - rho), 1.0)


def copies_in(pairs, sems):
    made = [
        [pltpu.make_async_copy(src, dst, sems.at[i, k]) for k, (src, dst) in enumerate(group)]
        for i, group in enumerate(pairs)
    ]
    for group in made:
        for copy in group:
            copy.start()
    return made


def step_kernel(iteration, kept, *refs):
    first = iteration == 0
    if first:
        (info, left, right, gathered, d_own, d_side, x_own, x_side, state_out, v_out, w_out, part,
         t_high, t_low, d_buf, v_buf, w_buf, in_sems, out_sems) = refs
        state = None
    else:
        (info, left, right, gathered, d_own, d_side, v_in, w_in, state, state_out, v_out, w_out, part,
         t_high, t_low, d_buf, v_buf, w_buf, in_sems, out_sems) = refs

    def side(own, sides, block):
        return own if block == 1 else sides.at[block // 2]

    loads = []
    for block in range(3):
        group = [(side(d_own, d_side, block), d_buf.at[block])]
        if first:
            group.append((side(x_own, x_side, block), v_buf.at[block]))
        else:
            group += [(v_in.at[block], v_buf.at[block]), (w_in.at[block], w_buf.at[block])]
        loads.append(group)
    loads = copies_in(loads, in_sems)

    scal = scalars(first, global_sums(info, gathered, ROWS + PIECE), None if first else state)
    rho = scal[5]
    state_out[...] = state_rows(first, scal, state, iteration)
    old_rho = None if first else state[0:1, 0:1]
    stores = []
    for block in (0, 2, 1):
        for copy in loads[block]:
            copy.wait()
        for z in range(ZS):
            rows = pl.ds(z * PIECE, PIECE)
            if block == 1:
                halves = [gathered[CORES * z + c, ROWS : ROWS + PIECE] for c in range(CORES)]
            else:
                halves = [gathered[CORES * z + block // 2, c * PIECE : (c + 1) * PIECE] for c in range(CORES)]
            image = jnp.concatenate(halves, axis=1)
            diag = d_buf[block, rows]
            if first:
                v, w = combine(True, scal, None, None, v_buf[block, rows], image)
            else:
                v, w = v_buf[block, rows], w_buf[block, rows]
                v, w = combine(False, scal, v, w, trial(v, w, diag, old_rho)[1], image)
            t = trial(v, w, diag, rho)[1]
            v_buf[block, rows] = v
            w_buf[block, rows] = w
            t_high[block, rows], t_low[block, rows] = split(t)
        if block in kept:
            at = kept.index(block)
            for k, (buf, out) in enumerate(((v_buf, v_out), (w_buf, w_out))):
                copy = pltpu.make_async_copy(buf.at[block], out.at[at], out_sems.at[k, at])
                copy.start()
                stores.append(copy)
    v_own = v_buf[1]
    r_own, t_own = trial(v_own, w_buf[1], d_buf[1], rho)
    apply_terms(info, left, right, t_high, t_low, t_own, v_own, r_own, part)
    for copy in stores:
        copy.wait()


def last_kernel(factor, info, gathered, d_own, v_in, w_in, state, wave, image, state_out):
    scal = scalars(False, global_sums(info, gathered, PIECE), state)
    state_out[...] = state_rows(False, scal, state, ITERS)
    old_rho = state[0:1, 0:1]
    for z in range(ZS):
        rows = pl.ds(z * PIECE, PIECE)
        got = jnp.concatenate([gathered[CORES * z + c, :PIECE] for c in range(CORES)], axis=1)
        v, w = v_in[0, rows], w_in[0, rows]
        v, w = combine(False, scal, v, w, trial(v, w, d_own[rows], old_rho)[1], got)
        wave[0, rows] = v * factor
        image[0, rows] = w * factor


def shape(*dims):
    return jax.ShapeDtypeStruct(dims, F32)


PARAMS = pltpu.CompilerParams(vmem_limit_bytes=24 * 1024 * 1024)
SPLITS = [pltpu.VMEM((3, M, M), BF16), pltpu.VMEM((3, M, M), BF16)]
PART = shape(ZS, ROWS + SCAL, LANES)


def run_first(info, left, right, x_own, x_side):
    return pl.pallas_call(
        first_kernel,
        out_shape=PART,
        in_specs=[SMEM] + [VMEM] * 4,
        out_specs=VMEM,
        scratch_shapes=SPLITS,
        compiler_params=PARAMS,
        name="first",
    )(info, left, right, x_own, x_side)


def run_step(iteration, info, left, right, gathered, *arrays):
    kept = (0, 1, 2) if iteration < ITERS - 1 else (1,)

    def body(*refs):
        step_kernel(iteration, kept, *refs)

    state = [] if iteration == 0 else [VMEM]
    return pl.pallas_call(
        body,
        out_shape=(shape(SCAL, 128), shape(len(kept), M, M), shape(len(kept), M, M), PART),
        in_specs=[SMEM] + [VMEM] * 3 + [HBM] * 4 + state,
        out_specs=(VMEM, HBM, HBM, VMEM),
        scratch_shapes=SPLITS + [pltpu.VMEM((3, M, M), F32)] * 3 + [
            pltpu.SemaphoreType.DMA((3, 3)), pltpu.SemaphoreType.DMA((2, 3))],
        compiler_params=PARAMS,
        name="step",
    )(info, left, right, gathered, *arrays)


def run_last(info, *arrays):
    factor = math.sqrt(BLOCKS * M * M)

    def body(*refs):
        last_kernel(factor, *refs)

    return pl.pallas_call(
        body,
        out_shape=(shape(1, M, M), shape(1, M, M), shape(SCAL, 128)),
        in_specs=[SMEM] + [VMEM] * 5,
        out_specs=(VMEM,) * 3,
        compiler_params=PARAMS,
        name="last",
    )(info, *arrays)


def halo_pairs():
    pairs = []
    for z in range(ZS):
        for core in range(CORES):
            for b in range(BLOCKS):
                source = b - 1 if core == 0 else b + 1
                if 0 <= source < BLOCKS:
                    base = (z * CORES + core) * BLOCKS
                    pairs.append((base + source, base + b))
    return pairs


def spread_pairs(slot):
    pairs = []
    for z in range(ZS):
        for core in range(CORES):
            for b in range(BLOCKS):
                y = (b // XS + z + slot * (YS // 2)) % YS
                x = (b % XS + core + 2 * slot) % XS
                base = (z * CORES + core) * BLOCKS
                pairs.append((base + y * XS + x, base + b))
    return pairs


def halo_whole(block):
    got = lax.ppermute(block, ALL, halo_pairs())
    return lax.all_gather(got, "core", axis=0)


def exchange(part, with_halo):
    pieces = lax.all_to_all(part, "z", 0, 0, tiled=True)
    both = lax.all_gather(jnp.sum(pieces, axis=0), "core", axis=0)
    mine = both[0] + both[1]
    rows, scal = mine[:ROWS], mine[ROWS:]
    parts = []
    if with_halo:
        parts.append(lax.ppermute(rows, ALL, halo_pairs()))
    parts.append(lax.dynamic_slice_in_dim(rows, lax.axis_index("core") * PIECE, PIECE, 0))
    parts += [lax.ppermute(scal, ALL, spread_pairs(slot)) for slot in range(2)]
    return lax.all_gather(jnp.concatenate(parts, axis=0), TERM, axis=0)


def per_device(start, diagonal, left_ops, right_ops, offsets, sizes):
    left, right = left_ops[:, 0], right_ops[:, 0]
    info = jnp.concatenate([lax.axis_index("block")[None].astype(jnp.int32), sizes, offsets[:, 0]])
    live = jnp.arange(M, dtype=jnp.int32) < sizes[0]
    x_own = jnp.where(live[:, None] & live[None, :], start[0], 0.0)
    x_side = halo_whole(x_own)
    part = run_first(info, left, right, x_own, x_side)
    d_own = diagonal[0]
    d_side = halo_whole(d_own)
    gathered = exchange(part, True)
    state, v, w, part = run_step(0, info, left, right, gathered, d_own, d_side, x_own, x_side)
    for iteration in range(1, ITERS):
        gathered = exchange(part, True)
        state, v, w, part = run_step(iteration, info, left, right, gathered, d_own, d_side, v, w, state)
    gathered = exchange(part, False)
    wave, image, state = run_last(info, gathered, d_own, v, w, state)
    return wave, image, state[2 : 2 + ITERS, 0]


def solution(mesh):
    grid = Mesh(np.asarray(mesh.devices).reshape(ZS, CORES, BLOCKS), ALL)
    return jax.shard_map(
        per_device,
        mesh=grid,
        in_specs=(
            P("block", None, None),
            P("block", None, None),
            P(TERM, "block", None, None),
            P(TERM, "block", None, None),
            P(TERM, "block"),
            P("block"),
        ),
        out_specs=(P("block", None, None), P("block", None, None), P()),
        check_vma=False,
    )
```

```python
import math

import jax
import jax.numpy as jnp
import numpy as np
from jax import lax
from jax.experimental import pallas as pl
from jax.experimental.pallas import tpu as pltpu
from jax.sharding import Mesh, PartitionSpec as P

ITERS = 3
ZS, CORES, BLOCKS = 8, 2, 32
GROUP = ZS * CORES
M = 256
PIECE = M // ZS
LANES = M // CORES
ROWS = PIECE * CORES
SCAL = 8
XS = 4
YS = BLOCKS // XS
TERM = ("z", "core")
ALL = ("z", "core", "block")
VMEM = pl.BlockSpec(memory_space=pltpu.VMEM)
SMEM = pl.BlockSpec(memory_space=pltpu.SMEM)
BF16, F32 = jnp.bfloat16, jnp.float32


def split(x):
    high = x.astype(BF16)
    return high, (x - high.astype(F32)).astype(BF16)


def dot3(a, b):
    def mm(x, y):
        return lax.dot_general(x, y, (((1,), (0,)), ((), ())), preferred_element_type=F32)

    return mm(a[0], b[0]) + (mm(a[0], b[1]) + mm(a[1], b[0]))


def column_sum(x):
    folded = x[:, :LANES] + x[:, LANES:]
    return jnp.sum(folded, axis=0, keepdims=True)


def apply_terms(info, left, right, t_high, t_low, t_own, v_own, r_own, part):
    total = jnp.zeros((M, M), F32)
    for term in range(left.shape[0]):
        sel = 1 - info[2 + term]
        half = dot3(split(left[term]), (t_high[sel], t_low[sel]))
        total = total + dot3(split(half), split(right[term]))
    size = info[1]
    live = (lax.broadcasted_iota(jnp.int32, (M, M), 0) < size) & (
        lax.broadcasted_iota(jnp.int32, (M, M), 1) < size
    )
    total = jnp.where(live, total, 0.0)
    share = 1.0 / GROUP
    rows = [
        column_sum(t_own * t_own) * share,
        column_sum(t_own * total),
    ]
    if v_own is not None:
        rows += [
            column_sum(v_own * t_own) * share,
            column_sum(t_own * r_own) * share,
            column_sum(v_own * total),
        ]
    rows.append(jnp.zeros((SCAL - len(rows), LANES), F32))
    scal = jnp.concatenate(rows, axis=0)
    for z in range(ZS):
        for core in range(CORES):
            part[z, core * PIECE : (core + 1) * PIECE] = total[
                z * PIECE : (z + 1) * PIECE, core * LANES : (core + 1) * LANES]
        part[z, ROWS:] = scal


def first_kernel(info, left, right, own, x_side, part, t_high, t_low):
    t_high[0], t_low[0] = split(x_side[0])
    t_high[1], t_low[1] = split(own[0])
    t_high[2], t_low[2] = split(x_side[1])
    apply_terms(info, left, right, t_high, t_low, own[0], None, None, part)


def global_sums(info, gathered, row):
    y, x = lax.shift_right_logical(info[0], 2), info[0] & (XS - 1)
    total = None
    for block in range(BLOCKS):
        far = (block % XS - x) & (XS - 1)
        slot = lax.shift_right_logical(far, 1)
        z = (block // XS - y - slot * (YS // 2)) & (YS - 1)
        at = pl.ds(pl.multiple_of(row + SCAL * slot, SCAL), SCAL)
        piece = gathered[CORES * z + (far & 1), at]
        total = piece if total is None else total + piece
    return jnp.sum(total, axis=1, keepdims=True)


def scalars(first, sums, state):
    tt, th = sums[0:1], sums[1:2]
    if first:
        scale = tt + 1e-12
        return None, jnp.sqrt(scale), None, None, None, th / scale, tt / scale, None
    p, tr, vh = sums[2:3], sums[3:4], sums[4:5]
    rho, vv = state[0:1, 0:1], state[1:2, 0:1]
    norm_sq = jnp.maximum(tt - 2.0 * p * p + p * p * vv, 0.0)
    n_sq = norm_sq + 1e-12
    n = jnp.sqrt(n_sq)
    tw = tr + rho * p
    coupling = tr / n
    curvature = (th - p * tw - p * vh + p * p * rho) / n_sq
    lowest = 0.5 * (rho + curvature) - jnp.sqrt((0.5 * (rho - curvature)) ** 2 + coupling * coupling)
    gap = curvature - lowest
    len_sq = gap * gap + coupling * coupling
    length = jnp.sqrt(len_sq)
    v_image = (vh - p * rho) / n
    v_unit = (p - p * vv) / n
    unit_sq = norm_sq / n_sq
    next_rho = (gap * gap * rho - gap * coupling * (v_image + coupling) + coupling * coupling * curvature) / len_sq
    next_vv = (gap * gap * vv - 2.0 * gap * coupling * v_unit + coupling * coupling * unit_sq) / len_sq
    return p, n, gap, coupling, length, next_rho, next_vv, lowest


def combine(first, scal, v, w, t, y):
    p, n, gap, coupling, length = scal[:5]
    if first:
        return t / n, y / n
    by_unit = coupling / (n * length)
    by_old = gap / length + p * by_unit
    return by_old * v - by_unit * t, by_old * w - by_unit * y


def state_rows(first, scal, state, iteration):
    rows = [scal[5], scal[6]]
    for i in range(ITERS):
        if i < iteration - 1:
            rows.append(state[2 + i : 3 + i, 0:1])
        elif i == iteration - 1 and not first:
            rows.append(scal[7])
        else:
            rows.append(jnp.zeros((1, 1), F32))
    rows.append(jnp.zeros((SCAL - len(rows), 1), F32))
    return jnp.broadcast_to(jnp.concatenate(rows, axis=0), (SCAL, 128))


def trial(v, w, diag, rho):
    r = w - rho * v
    return r, r / jnp.maximum(jnp.abs(diag - rho), 1.0)


def step_kernel(iteration, *refs):
    first = iteration == 0
    if first:
        (info, left, right, gathered, own, x_side, d_side, state_out, out, part, t_high, t_low) = refs
        old = state = None
    else:
        (info, left, right, gathered, own, x_side, d_side, old, state, state_out, out, part, t_high, t_low) = refs
    scal = scalars(first, global_sums(info, gathered, ROWS + PIECE), None if first else state)
    rho = scal[5]
    state_out[...] = state_rows(first, scal, state, iteration)
    old_rho = None if first else state[0:1, 0:1]
    for block in (0, 2, 1):
        for z in range(ZS):
            rows = pl.ds(z * PIECE, PIECE)
            if block == 1:
                halves = [gathered[CORES * z + c, ROWS : ROWS + PIECE] for c in range(CORES)]
                x, diag = own[0, rows], own[1, rows]
            else:
                halves = [gathered[CORES * z + block // 2, c * PIECE : (c + 1) * PIECE] for c in range(CORES)]
                x, diag = x_side[block // 2, rows], d_side[block // 2, rows]
            image = jnp.concatenate(halves, axis=1)
            if first:
                v, w = combine(True, scal, None, None, x, image)
            else:
                v, w = old[block, rows], old[3 + block, rows]
                v, w = combine(False, scal, v, w, trial(v, w, diag, old_rho)[1], image)
            t = trial(v, w, diag, rho)[1]
            out[block, rows] = v
            out[3 + block, rows] = w
            t_high[block, rows], t_low[block, rows] = split(t)
    v_own = out[1]
    r_own, t_own = trial(v_own, out[4], own[1], rho)
    apply_terms(info, left, right, t_high, t_low, t_own, v_own, r_own, part)


def last_kernel(factor, info, gathered, own, old, state, wave, image, energies):
    scal = scalars(False, global_sums(info, gathered, PIECE), state)
    rows = state_rows(False, scal, state, ITERS)
    for i in range(ITERS):
        energies[i] = rows[2 + i, 0]
    old_rho = state[0:1, 0:1]
    for z in range(ZS):
        rows = pl.ds(z * PIECE, PIECE)
        got = jnp.concatenate([gathered[CORES * z + c, :PIECE] for c in range(CORES)], axis=1)
        v, w = old[1, rows], old[4, rows]
        v, w = combine(False, scal, v, w, trial(v, w, own[1, rows], old_rho)[1], got)
        wave[0, rows] = v * factor
        image[0, rows] = w * factor


def shape(*dims):
    return jax.ShapeDtypeStruct(dims, F32)


PARAMS = pltpu.CompilerParams(vmem_limit_bytes=16 * 1024 * 1024)
SPLITS = [pltpu.VMEM((3, M, M), BF16), pltpu.VMEM((3, M, M), BF16)]
PART = shape(ZS, ROWS + SCAL, LANES)


def run_first(info, left, right, own, x_side):
    return pl.pallas_call(
        first_kernel,
        out_shape=PART,
        in_specs=[SMEM] + [VMEM] * 4,
        out_specs=VMEM,
        scratch_shapes=SPLITS,
        compiler_params=PARAMS,
        name="first",
    )(info, left, right, own, x_side)


def run_step(iteration, info, *arrays):
    def body(*refs):
        step_kernel(iteration, *refs)

    return pl.pallas_call(
        body,
        out_shape=(shape(SCAL, 128), shape(6, M, M), PART),
        in_specs=[SMEM] + [VMEM] * len(arrays),
        out_specs=(VMEM,) * 3,
        scratch_shapes=SPLITS,
        input_output_aliases={7: 1} if iteration else {},
        compiler_params=PARAMS,
        name="step",
    )(info, *arrays)


def run_last(info, *arrays):
    factor = math.sqrt(BLOCKS * M * M)

    def body(*refs):
        last_kernel(factor, *refs)

    return pl.pallas_call(
        body,
        out_shape=(shape(1, M, M), shape(1, M, M), shape(ITERS)),
        in_specs=[SMEM] + [VMEM] * 4,
        out_specs=(VMEM, VMEM, SMEM),
        compiler_params=PARAMS,
        name="last",
    )(info, *arrays)


def halo_pairs():
    pairs = []
    for z in range(ZS):
        for core in range(CORES):
            for b in range(BLOCKS):
                source = b - 1 if core == 0 else b + 1
                if 0 <= source < BLOCKS:
                    base = (z * CORES + core) * BLOCKS
                    pairs.append((base + source, base + b))
    return pairs


def spread_pairs(slot):
    pairs = []
    for z in range(ZS):
        for core in range(CORES):
            for b in range(BLOCKS):
                y = (b // XS + z + slot * (YS // 2)) % YS
                x = (b % XS + core + 2 * slot) % XS
                base = (z * CORES + core) * BLOCKS
                pairs.append((base + y * XS + x, base + b))
    return pairs


def halo_whole(blocks):
    got = lax.ppermute(blocks, ALL, halo_pairs())
    return [lax.all_gather(got[i], "core", axis=0) for i in range(2)]


def exchange(part, with_halo):
    pieces = lax.all_to_all(part, "z", 0, 0, tiled=True)
    both = lax.all_gather(sum(pieces[z] for z in range(1, ZS)) + pieces[0], "core", axis=0)
    mine = both[0] + both[1]
    rows, scal = mine[:ROWS], mine[ROWS:]
    parts = []
    if with_halo:
        parts.append(lax.ppermute(rows, ALL, halo_pairs()))
    parts.append(lax.dynamic_slice_in_dim(rows, lax.axis_index("core") * PIECE, PIECE, 0))
    parts += [lax.ppermute(scal, ALL, spread_pairs(slot)) for slot in range(2)]
    return lax.all_gather(jnp.concatenate(parts, axis=0), TERM, axis=0)


def per_device(start, diagonal, left_ops, right_ops, offsets, sizes):
    left, right = left_ops[:, 0], right_ops[:, 0]
    info = jnp.concatenate([lax.axis_index("block")[None].astype(jnp.int32), sizes, offsets[:, 0]])
    live = jnp.arange(M, dtype=jnp.int32) < sizes[0]
    own = jnp.stack([jnp.where(live[:, None] & live[None, :], start[0], 0.0), diagonal[0]])
    x_side, d_side = halo_whole(own)
    part = run_first(info, left, right, own, x_side)
    gathered = exchange(part, True)
    state, pair, part = run_step(0, info, left, right, gathered, own, x_side, d_side)
    for iteration in range(1, ITERS):
        gathered = exchange(part, True)
        state, pair, part = run_step(iteration, info, left, right, gathered, own, x_side, d_side, pair, state)
    gathered = exchange(part, False)
    wave, image, energies = run_last(info, gathered, own, pair, state)
    return wave, image, energies


def solution(mesh):
    grid = Mesh(np.asarray(mesh.devices).reshape(ZS, CORES, BLOCKS), ALL)
    return jax.shard_map(
        per_device,
        mesh=grid,
        in_specs=(
            P("block", None, None),
            P("block", None, None),
            P(TERM, "block", None, None),
            P(TERM, "block", None, None),
            P(TERM, "block"),
            P("block"),
        ),
        out_specs=(P("block", None, None), P("block", None, None), P()),
        check_vma=False,
    )
```

```python
import math

import jax
import jax.numpy as jnp
import numpy as np
from jax import lax
from jax.experimental import pallas as pl
from jax.experimental.pallas import tpu as pltpu
from jax.sharding import Mesh, PartitionSpec as P

ITERS = 3
ZS, CORES, BLOCKS = 8, 2, 32
GROUP = ZS * CORES
M = 256
PIECE = M // ZS
LANES = M // CORES
ROWS = PIECE * CORES
SCAL = 8
XS = 4
YS = BLOCKS // XS
TERM = ("z", "core")
BLOCK = ("y", "xh", "xl")
ALL = TERM + BLOCK
VMEM = pl.BlockSpec(memory_space=pltpu.VMEM)
SMEM = pl.BlockSpec(memory_space=pltpu.SMEM)
BF16, F32 = jnp.bfloat16, jnp.float32


def split(x):
    high = x.astype(BF16)
    return high, (x - high.astype(F32)).astype(BF16)


def dot3(a, b):
    def mm(x, y):
        return lax.dot_general(x, y, (((1,), (0,)), ((), ())), preferred_element_type=F32)

    return mm(a[0], b[0]) + (mm(a[0], b[1]) + mm(a[1], b[0]))


def column_sum(x):
    folded = x[:, :LANES] + x[:, LANES:]
    return jnp.sum(folded, axis=0, keepdims=True)


def prepare_kernel(left, right, left_high, left_low, right_high, right_low):
    for term in range(left.shape[0]):
        left_high[term], left_low[term] = split(left[term])
        right_high[term], right_low[term] = split(right[term])


def apply_terms(info, ops, t_high, t_low, t_own, v_own, r_own, part):
    total = jnp.zeros((M, M), F32)
    left_high, left_low, right_high, right_low = ops
    for term in range(left_high.shape[0]):
        sel = 1 - info[2 + term]
        half = dot3((left_high[term], left_low[term]), (t_high[sel], t_low[sel]))
        total = total + dot3(split(half), (right_high[term], right_low[term]))
    size = info[1]
    live = (lax.broadcasted_iota(jnp.int32, (M, M), 0) < size) & (
        lax.broadcasted_iota(jnp.int32, (M, M), 1) < size
    )
    total = jnp.where(live, total, 0.0)
    share = 1.0 / GROUP
    rows = [
        column_sum(t_own * t_own) * share,
        column_sum(t_own * total),
    ]
    if v_own is not None:
        rows += [
            column_sum(v_own * t_own) * share,
            column_sum(t_own * r_own) * share,
            column_sum(v_own * total),
        ]
    rows.append(jnp.zeros((SCAL - len(rows), LANES), F32))
    scal = jnp.concatenate(rows, axis=0)
    for z in range(ZS):
        for core in range(CORES):
            part[z, core * PIECE : (core + 1) * PIECE] = total[
                z * PIECE : (z + 1) * PIECE, core * LANES : (core + 1) * LANES]
        part[z, ROWS:] = scal


def first_kernel(info, lh, ll, rh, rl, x_own, x_side, part, t_high, t_low):
    t_high[0], t_low[0] = split(x_side[0])
    t_high[1], t_low[1] = split(x_own[...])
    t_high[2], t_low[2] = split(x_side[1])
    apply_terms(info, (lh, ll, rh, rl), t_high, t_low, x_own[...], None, None, part)


def global_sums(info, gathered, row):
    y, xh = lax.shift_right_logical(info[0], 2), lax.shift_right_logical(info[0], 1) & 1
    total = None
    for pair in range(GROUP):
        member = CORES * ((pair // CORES - y) & (YS - 1)) + ((pair % CORES - xh) & 1)
        piece = gathered[member, row : row + SCAL]
        total = piece if total is None else total + piece
    return jnp.sum(total, axis=1, keepdims=True)


def scalars(first, sums, state):
    tt, th = sums[0:1], sums[1:2]
    if first:
        scale = tt + 1e-12
        return None, jnp.sqrt(scale), None, None, None, th / scale, tt / scale, None
    p, tr, vh = sums[2:3], sums[3:4], sums[4:5]
    rho, vv = state[0:1, 0:1], state[1:2, 0:1]
    norm_sq = jnp.maximum(tt - 2.0 * p * p + p * p * vv, 0.0)
    n_sq = norm_sq + 1e-12
    n = jnp.sqrt(n_sq)
    tw = tr + rho * p
    coupling = tr / n
    curvature = (th - p * tw - p * vh + p * p * rho) / n_sq
    lowest = 0.5 * (rho + curvature) - jnp.sqrt((0.5 * (rho - curvature)) ** 2 + coupling * coupling)
    gap = curvature - lowest
    len_sq = gap * gap + coupling * coupling
    length = jnp.sqrt(len_sq)
    v_image = (vh - p * rho) / n
    v_unit = (p - p * vv) / n
    unit_sq = norm_sq / n_sq
    next_rho = (gap * gap * rho - gap * coupling * (v_image + coupling) + coupling * coupling * curvature) / len_sq
    next_vv = (gap * gap * vv - 2.0 * gap * coupling * v_unit + coupling * coupling * unit_sq) / len_sq
    return p, n, gap, coupling, length, next_rho, next_vv, lowest


def combine(first, scal, v, w, t, y):
    p, n, gap, coupling, length = scal[:5]
    if first:
        return t / n, y / n
    by_unit = coupling / (n * length)
    by_old = gap / length + p * by_unit
    return by_old * v - by_unit * t, by_old * w - by_unit * y


def state_rows(first, scal, state, iteration):
    rows = [scal[5], scal[6]]
    for i in range(ITERS):
        if i < iteration - 1:
            rows.append(state[2 + i : 3 + i, 0:1])
        elif i == iteration - 1 and not first:
            rows.append(scal[7])
        else:
            rows.append(jnp.zeros((1, 1), F32))
    rows.append(jnp.zeros((SCAL - len(rows), 1), F32))
    return jnp.broadcast_to(jnp.concatenate(rows, axis=0), (SCAL, 128))


def trial(v, w, diag, rho):
    return (w - rho * v) / jnp.maximum(jnp.abs(diag - rho), 1.0)


def step_kernel(iteration, *refs):
    first = iteration == 0
    if first:
        (info, lh, ll, rh, rl, gathered, x_own, x_side, d_own, d_side, state_out, out, part, t_high, t_low) = refs
        old = state = None
    else:
        (info, lh, ll, rh, rl, gathered, d_own, d_side, old, state, state_out, out, part, t_high, t_low) = refs
    scal = scalars(first, global_sums(info, gathered, 3 * PIECE), None if first else state)
    rho = scal[5]
    state_out[...] = state_rows(first, scal, state, iteration)
    odd = info[0] & 1
    for block in (0, 2, 1):
        at = 0 if block == 1 else pl.multiple_of(PIECE * (2 - odd if block == 0 else 1 + odd), PIECE)
        for z in range(ZS):
            rows = pl.ds(z * PIECE, PIECE)
            halves = [gathered[CORES * z + c, pl.ds(at, PIECE)] for c in range(CORES)]
            diag = d_own[rows] if block == 1 else d_side[block // 2, rows]
            image = jnp.concatenate(halves, axis=1)
            if first:
                x = x_own[rows] if block == 1 else x_side[block // 2, rows]
                v, w = combine(True, scal, None, None, x, image)
            else:
                v, w, t = (old[3 * k + block, rows] for k in range(3))
                v, w = combine(False, scal, v, w, t, image)
            t = trial(v, w, diag, rho)
            out[block, rows] = v
            out[3 + block, rows] = w
            out[6 + block, rows] = t
            t_high[block, rows], t_low[block, rows] = split(t)
    v_own = out[1]
    apply_terms(info, (lh, ll, rh, rl), t_high, t_low, out[7], v_own, out[4] - rho * v_own, part)


def last_kernel(factor, info, gathered, old, state, wave, image, energies):
    scal = scalars(False, global_sums(info, gathered, PIECE), state)
    rows = state_rows(False, scal, state, ITERS)
    for i in range(ITERS):
        energies[i] = rows[2 + i, 0]
    for z in range(ZS):
        rows = pl.ds(z * PIECE, PIECE)
        got = jnp.concatenate([gathered[CORES * z + c, :PIECE] for c in range(CORES)], axis=1)
        v, w = combine(False, scal, old[1, rows], old[4, rows], old[7, rows], got)
        wave[0, rows] = v * factor
        image[0, rows] = w * factor


def shape(*dims):
    return jax.ShapeDtypeStruct(dims, F32)


PARAMS = pltpu.CompilerParams(vmem_limit_bytes=16 * 1024 * 1024)
SPLITS = [pltpu.VMEM((3, M, M), BF16), pltpu.VMEM((3, M, M), BF16)]
PART = shape(ZS, ROWS + SCAL, LANES)


def run_prepare(left, right):
    part = jax.ShapeDtypeStruct(left.shape, BF16)
    return pl.pallas_call(
        prepare_kernel,
        out_shape=(part,) * 4,
        in_specs=[VMEM] * 2,
        out_specs=(VMEM,) * 4,
        compiler_params=PARAMS,
        cost_estimate=pl.CostEstimate(flops=4 * left.size, bytes_accessed=16 * left.size, transcendentals=0),
        name="prepare",
    )(left, right)


def run_first(info, *arrays):
    return pl.pallas_call(
        first_kernel,
        out_shape=PART,
        in_specs=[SMEM] + [VMEM] * len(arrays),
        out_specs=VMEM,
        scratch_shapes=SPLITS,
        compiler_params=PARAMS,
        name="first",
    )(info, *arrays)


def run_step(iteration, info, *arrays):
    def body(*refs):
        step_kernel(iteration, *refs)

    return pl.pallas_call(
        body,
        out_shape=(shape(SCAL, 128), shape(9, M, M), PART),
        in_specs=[SMEM] + [VMEM] * len(arrays),
        out_specs=(VMEM,) * 3,
        scratch_shapes=SPLITS,
        input_output_aliases={8: 1} if iteration else {},
        compiler_params=PARAMS,
        name="step",
    )(info, *arrays)


def run_last(info, *arrays):
    factor = math.sqrt(BLOCKS * M * M)

    def body(*refs):
        last_kernel(factor, *refs)

    return pl.pallas_call(
        body,
        out_shape=(shape(1, M, M), shape(1, M, M), shape(ITERS)),
        in_specs=[SMEM] + [VMEM] * 3,
        out_specs=(VMEM, VMEM, SMEM),
        compiler_params=PARAMS,
        name="last",
    )(info, *arrays)


def halo_pairs():
    pairs = []
    for z in range(ZS):
        for core in range(CORES):
            for b in range(BLOCKS):
                source = b - 1 if core == 0 else b + 1
                if 0 <= source < BLOCKS:
                    base = (z * CORES + core) * BLOCKS
                    pairs.append((base + source, base + b))
    return pairs


def spread_pairs():
    pairs = []
    for z in range(ZS):
        for core in range(CORES):
            for b in range(BLOCKS):
                y, x = (b // XS + z) % YS, (b % XS + 2 * core) % XS
                base = (z * CORES + core) * BLOCKS
                pairs.append((base + y * XS + x, base + b))
    return pairs


def gather_core(block):
    return lax.all_gather(block, "core", axis=0)


def exchange(part, place, with_halo):
    pieces = lax.all_to_all(part, "z", 0, 0, tiled=True)
    summed = sum(pieces[z] for z in range(1, ZS)) + pieces[0]
    four = lax.all_gather(summed, ("xl", "core"), axis=0)
    low, high = four[0] + four[1], four[2] + four[3]
    spread = lax.ppermute(low[ROWS:] + high[ROWS:], ALL, spread_pairs())
    odd, core, edge = place

    def half(rows):
        return jnp.where(core, rows[PIECE:ROWS], rows[:PIECE])

    own = half(jnp.where(odd, high, low))
    parts = [own]
    if with_halo:
        parts.append(half(jnp.where(odd, low, high)))
        shifted = [[b, (b + 1) % BLOCKS] for b in range(1, BLOCKS, 2)]
        two = lax.all_gather(own, BLOCK, axis=0, axis_index_groups=shifted)
        parts.append(jnp.where(edge, 0.0, jnp.where(odd, two[1], two[0])))
    return lax.all_gather(jnp.concatenate(parts + [spread], axis=0), TERM, axis=0)


def per_device(start, diagonal, left_ops, right_ops, offsets, sizes):
    info = jnp.concatenate([lax.axis_index(BLOCK)[None].astype(jnp.int32), sizes, offsets[:, 0]])
    live = jnp.arange(M, dtype=jnp.int32) < sizes[0]
    x_own = jnp.where(live[:, None] & live[None, :], start[0], 0.0)
    d_own = diagonal[0]
    b = lax.axis_index(BLOCK)
    place = (lax.axis_index("xl") == 1, lax.axis_index("core") == 1, (b == 0) | (b == BLOCKS - 1))
    x_side, d_side, place = lax.optimization_barrier(
        (gather_core(lax.ppermute(x_own, ALL, halo_pairs())),
         gather_core(lax.ppermute(d_own, ALL, halo_pairs())), place))
    ops = run_prepare(left_ops[:, 0], right_ops[:, 0])
    part = run_first(info, *ops, x_own, x_side)
    gathered = exchange(part, place, True)
    state, kept, part = run_step(0, info, *ops, gathered, x_own, x_side, d_own, d_side)
    for iteration in range(1, ITERS):
        gathered = exchange(part, place, True)
        state, kept, part = run_step(iteration, info, *ops, gathered, d_own, d_side, kept, state)
    gathered = exchange(part, place, False)
    wave, image, energies = run_last(info, gathered, kept, state)
    return wave, image, energies


def solution(mesh):
    grid = Mesh(np.asarray(mesh.devices).reshape(ZS, CORES, YS, 2, 2), ALL)
    return jax.shard_map(
        per_device,
        mesh=grid,
        in_specs=(
            P(BLOCK, None, None),
            P(BLOCK, None, None),
            P(TERM, BLOCK, None, None),
            P(TERM, BLOCK, None, None),
            P(TERM, BLOCK),
            P(BLOCK),
        ),
        out_specs=(P(BLOCK, None, None), P(BLOCK, None, None), P()),
        check_vma=False,
    )
```

```python
import math

import jax
import jax.numpy as jnp
import numpy as np
from jax import lax
from jax.experimental import pallas as pl
from jax.experimental.pallas import tpu as pltpu
from jax.sharding import Mesh, PartitionSpec as P

ITERS = 3
ZS, CORES, BLOCKS = 8, 2, 32
GROUP = ZS * CORES
M = 256
PIECE = M // ZS
LANES = M // CORES
ROWS = PIECE * CORES
SCAL = 8
FIRST_SCALE = 2.0**-14
XS = 4
YS = BLOCKS // XS
TERM = ("z", "core")
BLOCK = ("y", "xh", "xl")
ALL = TERM + BLOCK
VMEM = pl.BlockSpec(memory_space=pltpu.VMEM)
SMEM = pl.BlockSpec(memory_space=pltpu.SMEM)
BF16, F32 = jnp.bfloat16, jnp.float32


def split(x):
    high = x.astype(BF16)
    return high, (x - high.astype(F32)).astype(BF16)


def dot3(a, b):
    def mm(x, y):
        return lax.dot_general(x, y, (((1,), (0,)), ((), ())), preferred_element_type=F32)

    return mm(a[0], b[0]) + (mm(a[0], b[1]) + mm(a[1], b[0]))


def column_sum(x):
    folded = x[:, :LANES] + x[:, LANES:]
    return jnp.sum(folded, axis=0, keepdims=True)


def prepare_kernel(left, right, left_high, left_low, right_high, right_low):
    for term in range(left.shape[0]):
        left_high[term], left_low[term] = split(left[term])
        right_high[term], right_low[term] = split(right[term])


def apply_terms(info, ops, t_high, t_low, t_own, v_own, r_own, part):
    total = jnp.zeros((M, M), F32)
    left_high, left_low, right_high, right_low = ops
    for term in range(left_high.shape[0]):
        sel = 1 - info[2 + term]
        half = dot3((left_high[term], left_low[term]), (t_high[sel], t_low[sel]))
        total = total + dot3(split(half), (right_high[term], right_low[term]))
    size = info[1]
    live = (lax.broadcasted_iota(jnp.int32, (M, M), 0) < size) & (
        lax.broadcasted_iota(jnp.int32, (M, M), 1) < size
    )
    total = jnp.where(live, total, 0.0)
    share = 1.0 / GROUP
    level = total if v_own is not None else total * FIRST_SCALE
    rows = [
        column_sum(t_own * t_own) * share,
        column_sum(t_own * total),
        column_sum(level * level),
    ]
    if v_own is not None:
        rows += [
            column_sum(v_own * t_own) * share,
            column_sum(t_own * r_own) * share,
            column_sum(v_own * total),
        ]
    rows.append(jnp.zeros((SCAL - len(rows), LANES), F32))
    scal = jnp.concatenate(rows, axis=0)
    for z in range(ZS):
        for core in range(CORES):
            part[z, core * PIECE : (core + 1) * PIECE] = total[
                z * PIECE : (z + 1) * PIECE, core * LANES : (core + 1) * LANES]
        part[z, ROWS:] = scal


def first_kernel(info, lh, ll, rh, rl, x_own, x_side, part, t_high, t_low):
    t_high[0], t_low[0] = split(x_side[0])
    t_high[1], t_low[1] = split(x_own[...])
    t_high[2], t_low[2] = split(x_side[1])
    apply_terms(info, (lh, ll, rh, rl), t_high, t_low, x_own[...], None, None, part)


def global_sums(info, gathered, row):
    y, xh = lax.shift_right_logical(info[0], 2), lax.shift_right_logical(info[0], 1) & 1
    total = None
    for pair in range(GROUP):
        member = CORES * ((pair // CORES - y) & (YS - 1)) + ((pair % CORES - xh) & 1)
        piece = gathered[member, row : row + SCAL]
        total = piece if total is None else total + piece
    return jnp.sum(total, axis=1, keepdims=True)


def scalars(first, sums, state):
    tt, th = sums[0:1], sums[1:2]
    reach = math.sqrt(GROUP) * jnp.sqrt(sums[2:3])
    if first:
        n_sq = tt + 1e-12
        n = jnp.sqrt(n_sq)
        rho, vv, lowest = th / n_sq, tt / n_sq, None
        bound = reach / n * (1.0 / FIRST_SCALE)
        weights = (n,)
    else:
        p, tr, vh = sums[3:4], sums[4:5], sums[5:6]
        rho, vv, bound, scale = (state[i : i + 1, 0:1] for i in range(4))
        norm_sq = jnp.maximum(tt - 2.0 * p * p + p * p * vv, 0.0)
        n_sq = norm_sq + jnp.maximum(1e-12 * (scale * scale), 1e-36)
        n = jnp.sqrt(n_sq)
        tw = tr + rho * p
        coupling = tr / n
        curvature = (th - p * tw - p * vh + p * p * rho) / n_sq
        lowest = 0.5 * (rho + curvature) - jnp.sqrt((0.5 * (rho - curvature)) ** 2 + coupling * coupling)
        gap = curvature - lowest
        length = jnp.sqrt(gap * gap + coupling * coupling)
        cos, sin = gap / length, coupling / length
        v_image = (vh - p * rho) / n
        v_unit = (p - p * vv) / n
        unit_sq = norm_sq / n_sq
        rho = cos * cos * rho - cos * sin * (v_image + coupling) + sin * sin * curvature
        vv = cos * cos * vv - 2.0 * cos * sin * v_unit + sin * sin * unit_sq
        by_unit = sin / n
        by_old = cos + p * by_unit
        bound = jnp.abs(by_old) * bound + jnp.abs(by_unit) * reach
        weights = (by_old, by_unit)
    scale = 1.0 / jnp.maximum(bound + jnp.abs(rho) * jnp.sqrt(jnp.maximum(vv, 0.0)), 1.0)
    return weights, (rho, vv, bound, scale), lowest


def combine(weights, v, w, t, y):
    if len(weights) == 1:
        return t / weights[0], y / weights[0]
    by_old, by_unit = weights
    return by_old * v - by_unit * t, by_old * w - by_unit * y


def state_rows(now, lowest, state, iteration):
    rows = list(now)
    for i in range(ITERS):
        if i < iteration - 1:
            rows.append(state[4 + i : 5 + i, 0:1])
        elif i == iteration - 1:
            rows.append(lowest)
        else:
            rows.append(jnp.zeros((1, 1), F32))
    rows.append(jnp.zeros((SCAL - len(rows), 1), F32))
    return jnp.broadcast_to(jnp.concatenate(rows, axis=0), (SCAL, 128))


def trial(v, w, diag, rho, scale):
    return (w - rho * v) * scale / jnp.maximum(jnp.abs(diag - rho), 1.0)


def step_kernel(iteration, *refs):
    first = iteration == 0
    if first:
        (info, lh, ll, rh, rl, gathered, x_own, x_side, d_own, d_side, state_out, out, part, t_high, t_low) = refs
        old = state = None
    else:
        (info, lh, ll, rh, rl, gathered, d_own, d_side, old, state, state_out, out, part, t_high, t_low) = refs
    weights, now, lowest = scalars(first, global_sums(info, gathered, 3 * PIECE), state)
    rho, scale = now[0], now[3]
    state_out[...] = state_rows(now, lowest, state, iteration)
    odd = info[0] & 1
    for block in (0, 2, 1):
        at = 0 if block == 1 else pl.multiple_of(PIECE * (2 - odd if block == 0 else 1 + odd), PIECE)
        for z in range(ZS):
            rows = pl.ds(z * PIECE, PIECE)
            halves = [gathered[CORES * z + c, pl.ds(at, PIECE)] for c in range(CORES)]
            diag = d_own[rows] if block == 1 else d_side[block // 2, rows]
            image = jnp.concatenate(halves, axis=1)
            if first:
                x = x_own[rows] if block == 1 else x_side[block // 2, rows]
                v, w = combine(weights, None, None, x, image)
            else:
                v, w, t = (old[3 * k + block, rows] for k in range(3))
                v, w = combine(weights, v, w, t, image)
            t = trial(v, w, diag, rho, scale)
            out[block, rows] = v
            out[3 + block, rows] = w
            out[6 + block, rows] = t
            t_high[block, rows], t_low[block, rows] = split(t)
    v_own = out[1]
    apply_terms(info, (lh, ll, rh, rl), t_high, t_low, out[7], v_own, out[4] - rho * v_own, part)


def last_kernel(factor, info, gathered, old, state, wave, image, energies):
    weights, now, lowest = scalars(False, global_sums(info, gathered, PIECE), state)
    rows = state_rows(now, lowest, state, ITERS)
    for i in range(ITERS):
        energies[i] = rows[4 + i, 0]
    for z in range(ZS):
        rows = pl.ds(z * PIECE, PIECE)
        got = jnp.concatenate([gathered[CORES * z + c, :PIECE] for c in range(CORES)], axis=1)
        v, w = combine(weights, old[1, rows], old[4, rows], old[7, rows], got)
        wave[0, rows] = v * factor
        image[0, rows] = w * factor


def shape(*dims):
    return jax.ShapeDtypeStruct(dims, F32)


PARAMS = pltpu.CompilerParams(vmem_limit_bytes=16 * 1024 * 1024)
SPLITS = [pltpu.VMEM((3, M, M), BF16), pltpu.VMEM((3, M, M), BF16)]
PART = shape(ZS, ROWS + SCAL, LANES)


def run_prepare(left, right):
    part = jax.ShapeDtypeStruct(left.shape, BF16)
    return pl.pallas_call(
        prepare_kernel,
        out_shape=(part,) * 4,
        in_specs=[VMEM] * 2,
        out_specs=(VMEM,) * 4,
        compiler_params=PARAMS,
        cost_estimate=pl.CostEstimate(flops=4 * left.size, bytes_accessed=16 * left.size, transcendentals=0),
        name="prepare",
    )(left, right)


def run_first(info, *arrays):
    return pl.pallas_call(
        first_kernel,
        out_shape=PART,
        in_specs=[SMEM] + [VMEM] * len(arrays),
        out_specs=VMEM,
        scratch_shapes=SPLITS,
        compiler_params=PARAMS,
        name="first",
    )(info, *arrays)


def run_step(iteration, info, *arrays):
    def body(*refs):
        step_kernel(iteration, *refs)

    return pl.pallas_call(
        body,
        out_shape=(shape(SCAL, 128), shape(9, M, M), PART),
        in_specs=[SMEM] + [VMEM] * len(arrays),
        out_specs=(VMEM,) * 3,
        scratch_shapes=SPLITS,
        input_output_aliases={8: 1} if iteration else {},
        compiler_params=PARAMS,
        name="step",
    )(info, *arrays)


def run_last(info, *arrays):
    factor = math.sqrt(BLOCKS * M * M)

    def body(*refs):
        last_kernel(factor, *refs)

    return pl.pallas_call(
        body,
        out_shape=(shape(1, M, M), shape(1, M, M), shape(ITERS)),
        in_specs=[SMEM] + [VMEM] * 3,
        out_specs=(VMEM, VMEM, SMEM),
        compiler_params=PARAMS,
        name="last",
    )(info, *arrays)


def halo_pairs():
    pairs = []
    for z in range(ZS):
        for core in range(CORES):
            for b in range(BLOCKS):
                source = b - 1 if core == 0 else b + 1
                if 0 <= source < BLOCKS:
                    base = (z * CORES + core) * BLOCKS
                    pairs.append((base + source, base + b))
    return pairs


def spread_pairs():
    pairs = []
    for z in range(ZS):
        for core in range(CORES):
            for b in range(BLOCKS):
                y, x = (b // XS + z) % YS, XS - 1 - b % XS if core else b % XS
                base = (z * CORES + core) * BLOCKS
                pairs.append((base + y * XS + x, base + b))
    return pairs


def gather_core(block):
    return lax.all_gather(block, "core", axis=0)


def exchange(part, place, with_halo):
    pieces = lax.all_to_all(part, "z", 0, 0, tiled=True)
    summed = sum(pieces[z] for z in range(1, ZS)) + pieces[0]
    four = lax.all_gather(summed, ("xl", "core"), axis=0)
    low, high = four[0] + four[1], four[2] + four[3]
    spread = lax.ppermute(low[ROWS:] + high[ROWS:], ALL, spread_pairs())
    odd, core, edge = place

    def half(rows):
        return jnp.where(core, rows[PIECE:ROWS], rows[:PIECE])

    own = half(jnp.where(odd, high, low))
    parts = [own]
    if with_halo:
        parts.append(half(jnp.where(odd, low, high)))
        shifted = [[b, (b + 1) % BLOCKS] for b in range(1, BLOCKS, 2)]
        two = lax.all_gather(own, BLOCK, axis=0, axis_index_groups=shifted)
        parts.append(jnp.where(edge, 0.0, jnp.where(odd, two[1], two[0])))
    return lax.all_gather(jnp.concatenate(parts + [spread], axis=0), TERM, axis=0)


def per_device(start, diagonal, left_ops, right_ops, offsets, sizes):
    info = jnp.concatenate([lax.axis_index(BLOCK)[None].astype(jnp.int32), sizes, offsets[:, 0]])
    live = jnp.arange(M, dtype=jnp.int32) < sizes[0]
    x_own = jnp.where(live[:, None] & live[None, :], start[0], 0.0)
    d_own = diagonal[0]
    b = lax.axis_index(BLOCK)
    place = (lax.axis_index("xl") == 1, lax.axis_index("core") == 1, (b == 0) | (b == BLOCKS - 1))
    x_side, d_side, place = lax.optimization_barrier(
        (gather_core(lax.ppermute(x_own, ALL, halo_pairs())),
         gather_core(lax.ppermute(d_own, ALL, halo_pairs())), place))
    ops = run_prepare(left_ops[:, 0], right_ops[:, 0])
    part = run_first(info, *ops, x_own, x_side)
    gathered = exchange(part, place, True)
    state, kept, part = run_step(0, info, *ops, gathered, x_own, x_side, d_own, d_side)
    for iteration in range(1, ITERS):
        gathered = exchange(part, place, True)
        state, kept, part = run_step(iteration, info, *ops, gathered, d_own, d_side, kept, state)
    gathered = exchange(part, place, False)
    wave, image, energies = run_last(info, gathered, kept, state)
    return wave, image, energies


def solution(mesh):
    grid = Mesh(np.asarray(mesh.devices).reshape(ZS, CORES, YS, 2, 2), ALL)
    return jax.shard_map(
        per_device,
        mesh=grid,
        in_specs=(
            P(BLOCK, None, None),
            P(BLOCK, None, None),
            P(TERM, BLOCK, None, None),
            P(TERM, BLOCK, None, None),
            P(TERM, BLOCK),
            P(BLOCK),
        ),
        out_specs=(P(BLOCK, None, None), P(BLOCK, None, None), P()),
        check_vma=False,
    )
```

```python
import math

import jax
import jax.numpy as jnp
import numpy as np
from jax import lax
from jax.experimental import pallas as pl
from jax.experimental.pallas import tpu as pltpu
from jax.sharding import Mesh, PartitionSpec as P

ITERS = 3
ZS, CORES, BLOCKS = 8, 2, 32
GROUP = ZS * CORES
M = 256
PIECE = M // ZS
LANES = M // CORES
ROWS = PIECE * CORES
SCAL = 8
FIRST_SCALE = 2.0**-14
XS = 4
YS = BLOCKS // XS
TERM = ("z", "core")
BLOCK = ("y", "xh", "xl")
ALL = TERM + BLOCK
VMEM = pl.BlockSpec(memory_space=pltpu.VMEM)
SMEM = pl.BlockSpec(memory_space=pltpu.SMEM)
BF16, F32 = jnp.bfloat16, jnp.float32


def split(x):
    high = x.astype(BF16)
    return high, (x - high.astype(F32)).astype(BF16)


def dot3(a, b):
    def mm(x, y):
        return lax.dot_general(x, y, (((1,), (0,)), ((), ())), preferred_element_type=F32)

    return mm(a[0], b[0]) + (mm(a[0], b[1]) + mm(a[1], b[0]))


def column_sum(x):
    folded = x[:, :LANES] + x[:, LANES:]
    return jnp.sum(folded, axis=0, keepdims=True)


def prepare_kernel(left, right, left_high, left_low, right_high, right_low):
    left_high[0], left_low[0] = split(left[0])
    right_high[0], right_low[0] = split(right[0])


def apply_terms(info, ops, t_high, t_low, t_own, v_own, r_own, part):
    total = jnp.zeros((M, M), F32)
    left_high, left_low, right_high, right_low = ops
    for term in range(left_high.shape[0]):
        sel = 1 - info[2 + term]
        half = dot3((left_high[term], left_low[term]), (t_high[sel], t_low[sel]))
        total = total + dot3(split(half), (right_high[term], right_low[term]))
    size = info[1]
    live = (lax.broadcasted_iota(jnp.int32, (M, M), 0) < size) & (
        lax.broadcasted_iota(jnp.int32, (M, M), 1) < size
    )
    total = jnp.where(live, total, 0.0)
    share = 1.0 / GROUP
    level = total if v_own is not None else total * FIRST_SCALE
    rows = [
        column_sum(t_own * t_own) * share,
        column_sum(t_own * total),
        column_sum(level * level),
    ]
    if v_own is not None:
        rows += [
            column_sum(v_own * t_own) * share,
            column_sum(t_own * r_own) * share,
            column_sum(v_own * total),
        ]
    rows.append(jnp.zeros((SCAL - len(rows), LANES), F32))
    scal = jnp.concatenate(rows, axis=0)
    for z in range(ZS):
        for core in range(CORES):
            part[z, core * PIECE : (core + 1) * PIECE] = total[
                z * PIECE : (z + 1) * PIECE, core * LANES : (core + 1) * LANES]
        part[z, ROWS:] = scal


def first_kernel(info, lh, ll, rh, rl, x_own, x_side, part, t_high, t_low):
    t_high[0], t_low[0] = split(x_side[0])
    t_high[1], t_low[1] = split(x_own[...])
    t_high[2], t_low[2] = split(x_side[1])
    apply_terms(info, (lh, ll, rh, rl), t_high, t_low, x_own[...], None, None, part)


def global_sums(info, gathered, row):
    y, xh = lax.shift_right_logical(info[0], 2), lax.shift_right_logical(info[0], 1) & 1
    total = None
    for pair in range(GROUP):
        member = CORES * ((pair // CORES - y) & (YS - 1)) + ((pair % CORES - xh) & 1)
        piece = gathered[member, row : row + SCAL]
        total = piece if total is None else total + piece
    return jnp.sum(total, axis=1, keepdims=True)


def scalars(first, sums, state):
    tt, th = sums[0:1], sums[1:2]
    reach = math.sqrt(GROUP) * jnp.sqrt(sums[2:3])
    if first:
        n_sq = tt + 1e-12
        n = jnp.sqrt(n_sq)
        rho, vv, lowest = th / n_sq, tt / n_sq, None
        bound = reach / n * (1.0 / FIRST_SCALE)
        weights = (n,)
    else:
        p, tr, vh = sums[3:4], sums[4:5], sums[5:6]
        rho, vv, bound, scale = (state[i : i + 1, 0:1] for i in range(4))
        norm_sq = jnp.maximum(tt - 2.0 * p * p + p * p * vv, 0.0)
        n_sq = norm_sq + jnp.maximum(1e-12 * (scale * scale), 1e-36)
        n = jnp.sqrt(n_sq)
        tw = tr + rho * p
        coupling = tr / n
        curvature = (th - p * tw - p * vh + p * p * rho) / n_sq
        lowest = 0.5 * (rho + curvature) - jnp.sqrt((0.5 * (rho - curvature)) ** 2 + coupling * coupling)
        gap = curvature - lowest
        length = jnp.sqrt(gap * gap + coupling * coupling)
        cos, sin = gap / length, coupling / length
        v_image = (vh - p * rho) / n
        v_unit = (p - p * vv) / n
        unit_sq = norm_sq / n_sq
        rho = cos * cos * rho - cos * sin * (v_image + coupling) + sin * sin * curvature
        vv = cos * cos * vv - 2.0 * cos * sin * v_unit + sin * sin * unit_sq
        by_unit = sin / n
        by_old = cos + p * by_unit
        bound = jnp.abs(by_old) * bound + jnp.abs(by_unit) * reach
        weights = (by_old, by_unit)
    scale = 1.0 / jnp.maximum(bound + jnp.abs(rho) * jnp.sqrt(jnp.maximum(vv, 0.0)), 1.0)
    return weights, (rho, vv, bound, scale), lowest


def combine(weights, v, w, t, y):
    if len(weights) == 1:
        return t / weights[0], y / weights[0]
    by_old, by_unit = weights
    return by_old * v - by_unit * t, by_old * w - by_unit * y


def state_rows(now, lowest, state, iteration):
    rows = list(now)
    for i in range(ITERS):
        if i < iteration - 1:
            rows.append(state[4 + i : 5 + i, 0:1])
        elif i == iteration - 1:
            rows.append(lowest)
        else:
            rows.append(jnp.zeros((1, 1), F32))
    rows.append(jnp.zeros((SCAL - len(rows), 1), F32))
    return jnp.broadcast_to(jnp.concatenate(rows, axis=0), (SCAL, 128))


def trial(v, w, diag, rho, scale):
    return (w - rho * v) * scale / jnp.maximum(jnp.abs(diag - rho), 1.0)


def step_kernel(iteration, *refs):
    first = iteration == 0
    if first:
        (info, lh, ll, rh, rl, gathered, x_own, x_side, d_own, d_side, state_out, out, part, t_high, t_low) = refs
        old = state = None
    else:
        (info, lh, ll, rh, rl, gathered, d_own, d_side, old, state, state_out, out, part, t_high, t_low) = refs
    weights, now, lowest = scalars(first, global_sums(info, gathered, 3 * PIECE), state)
    rho, scale = now[0], now[3]
    state_out[...] = state_rows(now, lowest, state, iteration)
    odd = info[0] & 1
    for block in (0, 2, 1):
        at = 0 if block == 1 else pl.multiple_of(PIECE * (2 - odd if block == 0 else 1 + odd), PIECE)
        for z in range(ZS):
            rows = pl.ds(z * PIECE, PIECE)
            halves = [gathered[CORES * z + c, pl.ds(at, PIECE)] for c in range(CORES)]
            diag = d_own[rows] if block == 1 else d_side[block // 2, rows]
            image = jnp.concatenate(halves, axis=1)
            if first:
                x = x_own[rows] if block == 1 else x_side[block // 2, rows]
                v, w = combine(weights, None, None, x, image)
            else:
                v, w, t = (old[3 * k + block, rows] for k in range(3))
                v, w = combine(weights, v, w, t, image)
            t = trial(v, w, diag, rho, scale)
            out[block, rows] = v
            out[3 + block, rows] = w
            out[6 + block, rows] = t
            t_high[block, rows], t_low[block, rows] = split(t)
    v_own = out[1]
    apply_terms(info, (lh, ll, rh, rl), t_high, t_low, out[7], v_own, out[4] - rho * v_own, part)


def last_kernel(factor, info, gathered, old, state, wave, image, energies):
    weights, now, lowest = scalars(False, global_sums(info, gathered, PIECE), state)
    rows = state_rows(now, lowest, state, ITERS)
    for i in range(ITERS):
        energies[i] = rows[4 + i, 0]
    for z in range(ZS):
        rows = pl.ds(z * PIECE, PIECE)
        got = jnp.concatenate([gathered[CORES * z + c, :PIECE] for c in range(CORES)], axis=1)
        v, w = combine(weights, old[1, rows], old[4, rows], old[7, rows], got)
        wave[0, rows] = v * factor
        image[0, rows] = w * factor


def shape(*dims):
    return jax.ShapeDtypeStruct(dims, F32)


PARAMS = pltpu.CompilerParams(vmem_limit_bytes=16 * 1024 * 1024)
SPLITS = [pltpu.VMEM((3, M, M), BF16), pltpu.VMEM((3, M, M), BF16)]
PART = shape(ZS, ROWS + SCAL, LANES)


def run_prepare(left, right):
    part = jax.ShapeDtypeStruct(left.shape, BF16)
    one = pl.BlockSpec((1, M, M), lambda term: (term, 0, 0))
    return pl.pallas_call(
        prepare_kernel,
        out_shape=(part,) * 4,
        grid=(left.shape[0],),
        in_specs=[one] * 2,
        out_specs=(one,) * 4,
        compiler_params=PARAMS,
        cost_estimate=pl.CostEstimate(flops=4 * left.size, bytes_accessed=16 * left.size, transcendentals=0),
        name="prepare",
    )(left, right)


def run_first(info, *arrays):
    return pl.pallas_call(
        first_kernel,
        out_shape=PART,
        in_specs=[SMEM] + [VMEM] * len(arrays),
        out_specs=VMEM,
        scratch_shapes=SPLITS,
        compiler_params=PARAMS,
        name="first",
    )(info, *arrays)


def run_step(iteration, info, *arrays):
    def body(*refs):
        step_kernel(iteration, *refs)

    return pl.pallas_call(
        body,
        out_shape=(shape(SCAL, 128), shape(9, M, M), PART),
        in_specs=[SMEM] + [VMEM] * len(arrays),
        out_specs=(VMEM,) * 3,
        scratch_shapes=SPLITS,
        input_output_aliases={8: 1} if iteration else {},
        compiler_params=PARAMS,
        name="step",
    )(info, *arrays)


def run_last(info, *arrays):
    factor = math.sqrt(BLOCKS * M * M)

    def body(*refs):
        last_kernel(factor, *refs)

    return pl.pallas_call(
        body,
        out_shape=(shape(1, M, M), shape(1, M, M), shape(ITERS)),
        in_specs=[SMEM] + [VMEM] * 3,
        out_specs=(VMEM, VMEM, SMEM),
        compiler_params=PARAMS,
        name="last",
    )(info, *arrays)


def halo_pairs():
    pairs = []
    for z in range(ZS):
        for core in range(CORES):
            for b in range(BLOCKS):
                source = b - 1 if core == 0 else b + 1
                if 0 <= source < BLOCKS:
                    base = (z * CORES + core) * BLOCKS
                    pairs.append((base + source, base + b))
    return pairs


def spread_pairs():
    pairs = []
    for z in range(ZS):
        for core in range(CORES):
            for b in range(BLOCKS):
                y, x = (b // XS + z) % YS, XS - 1 - b % XS if core else b % XS
                base = (z * CORES + core) * BLOCKS
                pairs.append((base + y * XS + x, base + b))
    return pairs


def gather_core(block):
    return lax.all_gather(block, "core", axis=0)


def exchange(part, place, with_halo):
    pieces = lax.all_to_all(part, "z", 0, 0, tiled=True)
    summed = sum(pieces[z] for z in range(1, ZS)) + pieces[0]
    four = lax.all_gather(summed, ("xl", "core"), axis=0)
    low, high = four[0] + four[1], four[2] + four[3]
    spread = lax.ppermute(low[ROWS:] + high[ROWS:], ALL, spread_pairs())
    odd, core, edge = place

    def half(rows):
        return jnp.where(core, rows[PIECE:ROWS], rows[:PIECE])

    own = half(jnp.where(odd, high, low))
    parts = [own]
    if with_halo:
        parts.append(half(jnp.where(odd, low, high)))
        shifted = [[b, (b + 1) % BLOCKS] for b in range(1, BLOCKS, 2)]
        two = lax.all_gather(own, BLOCK, axis=0, axis_index_groups=shifted)
        parts.append(jnp.where(edge, 0.0, jnp.where(odd, two[1], two[0])))
    return lax.all_gather(jnp.concatenate(parts + [spread], axis=0), TERM, axis=0)


def per_device(start, diagonal, left_ops, right_ops, offsets, sizes):
    info = jnp.concatenate([lax.axis_index(BLOCK)[None].astype(jnp.int32), sizes, offsets[:, 0]])
    live = jnp.arange(M, dtype=jnp.int32) < sizes[0]
    x_own = jnp.where(live[:, None] & live[None, :], start[0], 0.0)
    d_own = diagonal[0]
    b = lax.axis_index(BLOCK)
    place = (lax.axis_index("xl") == 1, lax.axis_index("core") == 1, (b == 0) | (b == BLOCKS - 1))
    x_side, d_side, place = lax.optimization_barrier(
        (gather_core(lax.ppermute(x_own, ALL, halo_pairs())),
         gather_core(lax.ppermute(d_own, ALL, halo_pairs())), place))
    ops = run_prepare(left_ops[:, 0], right_ops[:, 0])
    part = run_first(info, *ops, x_own, x_side)
    gathered = exchange(part, place, True)
    state, kept, part = run_step(0, info, *ops, gathered, x_own, x_side, d_own, d_side)
    for iteration in range(1, ITERS):
        gathered = exchange(part, place, True)
        state, kept, part = run_step(iteration, info, *ops, gathered, d_own, d_side, kept, state)
    gathered = exchange(part, place, False)
    wave, image, energies = run_last(info, gathered, kept, state)
    return wave, image, energies


def solution(mesh):
    grid = Mesh(np.asarray(mesh.devices).reshape(ZS, CORES, YS, 2, 2), ALL)
    return jax.shard_map(
        per_device,
        mesh=grid,
        in_specs=(
            P(BLOCK, None, None),
            P(BLOCK, None, None),
            P(TERM, BLOCK, None, None),
            P(TERM, BLOCK, None, None),
            P(TERM, BLOCK),
            P(BLOCK),
        ),
        out_specs=(P(BLOCK, None, None), P(BLOCK, None, None), P()),
        check_vma=False,
    )
```

```python
import math

import jax
import jax.numpy as jnp
import numpy as np
from jax import lax
from jax.experimental import pallas as pl
from jax.experimental.pallas import tpu as pltpu
from jax.sharding import Mesh, PartitionSpec as P

ITERS = 3
ZS, CORES, BLOCKS = 8, 2, 32
GROUP = ZS * CORES
M = 256
PIECE = M // ZS
LANES = M // CORES
ROWS = PIECE * CORES
SCAL = 8
FIRST_SCALE = 2.0**-14
XS = 4
YS = BLOCKS // XS
TERM = ("z", "core")
BLOCK = ("y", "xh", "xl")
ALL = TERM + BLOCK
VMEM = pl.BlockSpec(memory_space=pltpu.VMEM)
SMEM = pl.BlockSpec(memory_space=pltpu.SMEM)
BF16, F32 = jnp.bfloat16, jnp.float32


def split(x):
    high = x.astype(BF16)
    return high, (x - high.astype(F32)).astype(BF16)


def dot3(a, b):
    def mm(x, y):
        return lax.dot_general(x, y, (((1,), (0,)), ((), ())), preferred_element_type=F32)

    return mm(a[0], b[0]) + (mm(a[0], b[1]) + mm(a[1], b[0]))


def column_sum(x):
    folded = x[:, :LANES] + x[:, LANES:]
    return jnp.sum(folded, axis=0, keepdims=True)


def prepare_kernel(left, right, left_high, left_low, right_high, right_low):
    for term in range(left.shape[0]):
        left_high[term], left_low[term] = split(left[term])
        right_high[term], right_low[term] = split(right[term])


def apply_terms(info, ops, t_high, t_low, t_own, v_own, r_own, part):
    total = jnp.zeros((M, M), F32)
    left_high, left_low, right_high, right_low = ops
    for term in range(left_high.shape[0]):
        sel = 1 - info[2 + term]
        half = dot3((left_high[term], left_low[term]), (t_high[sel], t_low[sel]))
        total = total + dot3(split(half), (right_high[term], right_low[term]))
    size = info[1]
    live = (lax.broadcasted_iota(jnp.int32, (M, M), 0) < size) & (
        lax.broadcasted_iota(jnp.int32, (M, M), 1) < size
    )
    total = jnp.where(live, total, 0.0)
    share = 1.0 / GROUP
    level = total if v_own is not None else total * FIRST_SCALE
    rows = [
        column_sum(t_own * t_own) * share,
        column_sum(t_own * total),
        column_sum(level * level),
    ]
    if v_own is not None:
        rows += [
            column_sum(v_own * t_own) * share,
            column_sum(t_own * r_own) * share,
            column_sum(v_own * total),
        ]
    rows.append(jnp.zeros((SCAL - len(rows), LANES), F32))
    scal = jnp.concatenate(rows, axis=0)
    for z in range(ZS):
        for core in range(CORES):
            part[z, core * PIECE : (core + 1) * PIECE] = total[
                z * PIECE : (z + 1) * PIECE, core * LANES : (core + 1) * LANES]
        part[z, ROWS:] = scal


def first_kernel(info, lh, ll, rh, rl, x_own, x_side, part, t_high, t_low):
    t_high[0], t_low[0] = split(x_side[0])
    t_high[1], t_low[1] = split(x_own[...])
    t_high[2], t_low[2] = split(x_side[1])
    apply_terms(info, (lh, ll, rh, rl), t_high, t_low, x_own[...], None, None, part)


def global_sums(info, gathered, row):
    y, xh = lax.shift_right_logical(info[0], 2), lax.shift_right_logical(info[0], 1) & 1
    total = None
    for pair in range(GROUP):
        member = CORES * ((pair // CORES - y) & (YS - 1)) + ((pair % CORES - xh) & 1)
        piece = gathered[member, row : row + SCAL]
        total = piece if total is None else total + piece
    return jnp.sum(total, axis=1, keepdims=True)


def scalars(first, sums, state):
    tt, th = sums[0:1], sums[1:2]
    reach = math.sqrt(GROUP) * jnp.sqrt(sums[2:3])
    if first:
        n_sq = tt + 1e-12
        n = jnp.sqrt(n_sq)
        rho, vv, lowest = th / n_sq, tt / n_sq, None
        bound = reach / n * (1.0 / FIRST_SCALE)
        weights = (n,)
    else:
        p, tr, vh = sums[3:4], sums[4:5], sums[5:6]
        rho, vv, bound, scale = (state[i : i + 1, 0:1] for i in range(4))
        norm_sq = jnp.maximum(tt - 2.0 * p * p + p * p * vv, 0.0)
        n_sq = norm_sq + jnp.maximum(1e-12 * (scale * scale), 1e-36)
        n = jnp.sqrt(n_sq)
        tw = tr + rho * p
        coupling = tr / n
        curvature = (th - p * tw - p * vh + p * p * rho) / n_sq
        lowest = 0.5 * (rho + curvature) - jnp.sqrt((0.5 * (rho - curvature)) ** 2 + coupling * coupling)
        gap = curvature - lowest
        length = jnp.sqrt(gap * gap + coupling * coupling)
        cos, sin = gap / length, coupling / length
        v_image = (vh - p * rho) / n
        v_unit = (p - p * vv) / n
        unit_sq = norm_sq / n_sq
        rho = cos * cos * rho - cos * sin * (v_image + coupling) + sin * sin * curvature
        vv = cos * cos * vv - 2.0 * cos * sin * v_unit + sin * sin * unit_sq
        by_unit = sin / n
        by_old = cos + p * by_unit
        bound = jnp.abs(by_old) * bound + jnp.abs(by_unit) * reach
        weights = (by_old, by_unit)
    scale = 1.0 / jnp.maximum(bound + jnp.abs(rho) * jnp.sqrt(jnp.maximum(vv, 0.0)), 1.0)
    return weights, (rho, vv, bound, scale), lowest


def combine(weights, v, w, t, y):
    if len(weights) == 1:
        return t / weights[0], y / weights[0]
    by_old, by_unit = weights
    return by_old * v - by_unit * t, by_old * w - by_unit * y


def state_rows(now, lowest, state, iteration):
    rows = list(now)
    for i in range(ITERS):
        if i < iteration - 1:
            rows.append(state[4 + i : 5 + i, 0:1])
        elif i == iteration - 1:
            rows.append(lowest)
        else:
            rows.append(jnp.zeros((1, 1), F32))
    rows.append(jnp.zeros((SCAL - len(rows), 1), F32))
    return jnp.broadcast_to(jnp.concatenate(rows, axis=0), (SCAL, 128))


def trial(v, w, diag, rho, scale):
    return (w - rho * v) * scale / jnp.maximum(jnp.abs(diag - rho), 1.0)


def step_kernel(iteration, *refs):
    first = iteration == 0
    if first:
        (info, lh, ll, rh, rl, gathered, x_own, x_side, d_own, d_got, d_far, state_out, out, part, t_high, t_low) = refs
        old = state = None
    else:
        (info, lh, ll, rh, rl, gathered, d_own, d_got, d_far, old, state, state_out, out, part, t_high, t_low) = refs
    weights, now, lowest = scalars(first, global_sums(info, gathered, 3 * PIECE), state)
    rho, scale = now[0], now[3]
    state_out[...] = state_rows(now, lowest, state, iteration)
    odd = info[0] & 1
    for block in (0, 2, 1):
        at = 0 if block == 1 else pl.multiple_of(PIECE * (2 - odd if block == 0 else 1 + odd), PIECE)
        near = info[6] == block // 2
        for z in range(ZS):
            rows = pl.ds(z * PIECE, PIECE)
            halves = [gathered[CORES * z + c, pl.ds(at, PIECE)] for c in range(CORES)]
            diag = d_own[rows] if block == 1 else jnp.where(near, d_got[rows], d_far[rows])
            image = jnp.concatenate(halves, axis=1)
            if first:
                x = x_own[rows] if block == 1 else x_side[block // 2, rows]
                v, w = combine(weights, None, None, x, image)
            else:
                v, w, t = (old[3 * k + block, rows] for k in range(3))
                v, w = combine(weights, v, w, t, image)
            t = trial(v, w, diag, rho, scale)
            out[block, rows] = v
            out[3 + block, rows] = w
            out[6 + block, rows] = t
            t_high[block, rows], t_low[block, rows] = split(t)
    v_own = out[1]
    apply_terms(info, (lh, ll, rh, rl), t_high, t_low, out[7], v_own, out[4] - rho * v_own, part)


def last_kernel(factor, info, gathered, old, state, wave, image, energies):
    weights, now, lowest = scalars(False, global_sums(info, gathered, PIECE), state)
    rows = state_rows(now, lowest, state, ITERS)
    for i in range(ITERS):
        energies[i] = rows[4 + i, 0]
    for z in range(ZS):
        rows = pl.ds(z * PIECE, PIECE)
        got = jnp.concatenate([gathered[CORES * z + c, :PIECE] for c in range(CORES)], axis=1)
        v, w = combine(weights, old[1, rows], old[4, rows], old[7, rows], got)
        wave[0, rows] = v * factor
        image[0, rows] = w * factor


def shape(*dims):
    return jax.ShapeDtypeStruct(dims, F32)


PARAMS = pltpu.CompilerParams(vmem_limit_bytes=16 * 1024 * 1024)
SPLITS = [pltpu.VMEM((3, M, M), BF16), pltpu.VMEM((3, M, M), BF16)]
PART = shape(ZS, ROWS + SCAL, LANES)


def run_prepare(left, right):
    part = jax.ShapeDtypeStruct(left.shape, BF16)
    return pl.pallas_call(
        prepare_kernel,
        out_shape=(part,) * 4,
        in_specs=[VMEM] * 2,
        out_specs=(VMEM,) * 4,
        compiler_params=PARAMS,
        cost_estimate=pl.CostEstimate(flops=4 * left.size, bytes_accessed=16 * left.size, transcendentals=0),
        name="prepare",
    )(left, right)


def run_first(info, *arrays):
    return pl.pallas_call(
        first_kernel,
        out_shape=PART,
        in_specs=[SMEM] + [VMEM] * len(arrays),
        out_specs=VMEM,
        scratch_shapes=SPLITS,
        compiler_params=PARAMS,
        name="first",
    )(info, *arrays)


def run_step(iteration, info, *arrays):
    def body(*refs):
        step_kernel(iteration, *refs)

    return pl.pallas_call(
        body,
        out_shape=(shape(SCAL, 128), shape(9, M, M), PART),
        in_specs=[SMEM] + [VMEM] * len(arrays),
        out_specs=(VMEM,) * 3,
        scratch_shapes=SPLITS,
        input_output_aliases={9: 1} if iteration else {},
        compiler_params=PARAMS,
        name="step",
    )(info, *arrays)


def run_last(info, *arrays):
    factor = math.sqrt(BLOCKS * M * M)

    def body(*refs):
        last_kernel(factor, *refs)

    return pl.pallas_call(
        body,
        out_shape=(shape(1, M, M), shape(1, M, M), shape(ITERS)),
        in_specs=[SMEM] + [VMEM] * 3,
        out_specs=(VMEM, VMEM, SMEM),
        compiler_params=PARAMS,
        name="last",
    )(info, *arrays)


def halo_pairs():
    pairs = []
    for z in range(ZS):
        for core in range(CORES):
            for b in range(BLOCKS):
                source = b - 1 if core == 0 else b + 1
                if 0 <= source < BLOCKS:
                    base = (z * CORES + core) * BLOCKS
                    pairs.append((base + source, base + b))
    return pairs


def spread_pairs():
    pairs = []
    for z in range(ZS):
        for core in range(CORES):
            for b in range(BLOCKS):
                y, x = (b // XS + z) % YS, XS - 1 - b % XS if core else b % XS
                base = (z * CORES + core) * BLOCKS
                pairs.append((base + y * XS + x, base + b))
    return pairs


def gather_core(block):
    return lax.all_gather(block, "core", axis=0)


def exchange(part, place, with_halo):
    pieces = lax.all_to_all(part, "z", 0, 0, tiled=True)
    summed = sum(pieces[z] for z in range(1, ZS)) + pieces[0]
    four = lax.all_gather(summed, ("xl", "core"), axis=0)
    low, high = four[0] + four[1], four[2] + four[3]
    spread = lax.ppermute(low[ROWS:] + high[ROWS:], ALL, spread_pairs())
    odd, core, edge = place

    def half(rows):
        return jnp.where(core, rows[PIECE:ROWS], rows[:PIECE])

    own = half(jnp.where(odd, high, low))
    parts = [own]
    if with_halo:
        parts.append(half(jnp.where(odd, low, high)))
        shifted = [[b, (b + 1) % BLOCKS] for b in range(1, BLOCKS, 2)]
        two = lax.all_gather(own, BLOCK, axis=0, axis_index_groups=shifted)
        parts.append(jnp.where(edge, 0.0, jnp.where(odd, two[1], two[0])))
    return lax.all_gather(jnp.concatenate(parts + [spread], axis=0), TERM, axis=0)


def per_device(start, diagonal, left_ops, right_ops, offsets, sizes):
    info = jnp.concatenate([lax.axis_index(BLOCK)[None].astype(jnp.int32), sizes, offsets[:, 0],
                            lax.axis_index("core")[None].astype(jnp.int32)])
    live = jnp.arange(M, dtype=jnp.int32) < sizes[0]
    x_own = jnp.where(live[:, None] & live[None, :], start[0], 0.0)
    d_own = diagonal[0]
    b = lax.axis_index(BLOCK)
    place = (lax.axis_index("xl") == 1, lax.axis_index("core") == 1, (b == 0) | (b == BLOCKS - 1))
    x_side, d_got, place = lax.optimization_barrier(
        (gather_core(lax.ppermute(x_own, ALL, halo_pairs())), lax.ppermute(d_own, ALL, halo_pairs()), place))
    d_side = (d_got, lax.ppermute(d_got, "core", [(0, 1), (1, 0)]))
    ops = run_prepare(left_ops[:, 0], right_ops[:, 0])
    part = run_first(info, *ops, x_own, x_side)
    gathered = exchange(part, place, True)
    state, kept, part = run_step(0, info, *ops, gathered, x_own, x_side, d_own, *d_side)
    for iteration in range(1, ITERS):
        gathered = exchange(part, place, True)
        state, kept, part = run_step(iteration, info, *ops, gathered, d_own, *d_side, kept, state)
    gathered = exchange(part, place, False)
    wave, image, energies = run_last(info, gathered, kept, state)
    return wave, image, energies


def solution(mesh):
    grid = Mesh(np.asarray(mesh.devices).reshape(ZS, CORES, YS, 2, 2), ALL)
    return jax.shard_map(
        per_device,
        mesh=grid,
        in_specs=(
            P(BLOCK, None, None),
            P(BLOCK, None, None),
            P(TERM, BLOCK, None, None),
            P(TERM, BLOCK, None, None),
            P(TERM, BLOCK),
            P(BLOCK),
        ),
        out_specs=(P(BLOCK, None, None), P(BLOCK, None, None), P()),
        check_vma=False,
    )
```
